512 devices in a mesh: atm: 32 (over z_lo, x, core), ocn: 16 (over y, z_hi).
Axes of the slice: x: 4, y: 4, z: 16 (z_hi: 4, z_lo: 4; z = z_hi * 4 + z_lo), core: 2. Of those that a mesh axis runs over, the one named last changes fastest.
Arguments:
- sky_velocity_tensor: bfloat16 [32, 32, 128, 512], P('ocn', 'atm'), may hold values from -6 to 6
- marine_tensor: bfloat16 [32, 64, 256, 256], P(None, 'ocn', 'atm'), may hold values from -6 to 6
- above_rotation_quarters: int32 [32], P('atm'), may hold values from 0 to 3
- beneath_rotation_quarters: int32 [32], P('atm'), may hold values from 0 to 3
- covering_pixels: int32 [64, 256, 4], P('ocn', 'atm'), may hold values from 0 to 7
- marine_pixel_indicator: int32 [64, 256], P('ocn', 'atm'), may hold values 0 or 1
- sky_stencil_filter: float32 [9, 512], replicated, may hold values from -2 to 2
- sky_scale_factor: float32 [512], replicated, may hold values from 0.1 to 1.9
- marine_heat_matrix: float32 [8, 512], replicated, may hold values from -2 to 2
- sky_expansion_matrix: bfloat16 [512, 1024], replicated, may hold values from -0.25 to 0.25
- sky_projection_matrix: bfloat16 [1024, 512], replicated, may hold values from -0.1875 to 0.1875
- exchange_output_matrix: bfloat16 [512, 16], replicated, may hold values from -0.25 to 0.25
- marine_stencil_filter: float32 [9, 256], replicated, may hold values from -2 to 2
- marine_scale_factor: float32 [256], replicated, may hold values from 0.1 to 1.9
- exchange_into_marine_matrix: float32 [16, 256], replicated, may hold values from -1.5 to 1.5
- marine_expansion_matrix: bfloat16 [256, 512], replicated, may hold values from -0.375 to 0.375
- marine_projection_matrix: bfloat16 [512, 256], replicated, may hold values from -0.25 to 0.25
- marine_interface_matrix: bfloat16 [256, 8], replicated, may hold values from -0.375 to 0.375
Outputs:
- air_out: bfloat16 [32, 32, 128, 512], P('ocn', 'atm')
- ocean_out: bfloat16 [32, 64, 256, 256], P(None, 'ocn', 'atm')
The draws below stay inside these ranges and needn't reach their ends.
Inputs may be any that keep to these rules, and one draw needn't show every extreme that they name: `covering_pixels`: entries are indices m = row * 4 + column into the 2 x 4 atmosphere block under the ocean tile.
All inputs are finite; a program needn't handle non-finite values. No bound on the sum of `marine_pixel_indicator` on one device may be relied on, other than what follows from the above.
Results may differ from the reference program's by a relative error of at most 0.015.
Values may be sent and summed in bfloat16 or wider, within the bound.
A program may use at most 64 MiB of HBM per device.

```python
import jax
import jax.numpy as jnp
from jax import lax

SKY_LAYERS = 512
HA = 1024
CO = 256
HO = 512
NF = 16
MARINE_QUANTITY = 8
K = 4
NSTEP = 2
AC = 128
B = 32
AROWS = 32
OROWS = 64
OCOLS = 256
ORD = 4
OCD = 8
ABR = 2
ABC = 4
ABLK = 8


def set_ends(result, own_key, low, high):
    shape = result.shape
    place = [jax.random.randint(jax.random.fold_in(own_key, axis), (), 0, shape[axis]) for axis in range(len(shape))]
    result = result.at[tuple(place)].set(low)
    longest = shape.index(max(shape))
    place[longest] = (place[longest] + 1) % shape[longest]
    return result.at[tuple(place)].set(high)


def block_levels(rng, dims, pieces, smallest, largest):
    level = 1.0
    for dim, parts in pieces:
        steps = jax.random.uniform(jax.random.fold_in(jax.random.fold_in(rng, 6), dim), (parts,), jnp.float32, smallest / len(pieces), largest / len(pieces))
        level = level * jnp.repeat(jnp.exp(steps), dims[dim] // parts).reshape((-1,) + (1,) * (len(dims) - 1 - dim))
    return level


def centred(rng, dims, scale, limit, cuts=(), kind=jnp.bfloat16):
    values = jax.random.normal(rng, dims, jnp.float32) * scale
    if len(cuts) > 0:
        values = block_levels(rng, dims, cuts, -0.22, 0.18) * values
    return jnp.clip(values, min=-limit, max=limit).astype(kind)


def setup_inputs(seed: int = 0) -> dict:
    keys = jax.random.split(jax.random.key(seed), 19)
    return {
        "sky_velocity_tensor": centred(keys[0], (B, AROWS, AC, SKY_LAYERS), 1.0, 6.0, ((0, 16), (1, 32))),
        "marine_tensor": centred(keys[1], (B, OROWS, OCOLS, CO), 1.0, 6.0, ((1, 16), (2, 32))),
        "above_rotation_quarters": set_ends(jax.random.randint(keys[2], (AROWS,), 0, 4), jax.random.fold_in(keys[2], 1), 0, 3).astype(jnp.int32),
        "beneath_rotation_quarters": set_ends(jax.random.randint(keys[3], (AROWS,), 0, 4), jax.random.fold_in(keys[3], 1), 0, 3).astype(jnp.int32),
        "covering_pixels": set_ends(jax.random.randint(keys[4], (OROWS, OCOLS, K), 0, ABLK), jax.random.fold_in(keys[4], 1), 0, ABLK - 1).astype(jnp.int32),
        "marine_pixel_indicator": set_ends((jax.random.randint(keys[5], (OROWS, OCOLS), 0, 5) < 3).astype(jnp.int32), jax.random.fold_in(keys[5], 1), 0, 1),
        "sky_stencil_filter": centred(keys[6], (9, SKY_LAYERS), 0.33, 2.0, (), jnp.float32),
        "sky_scale_factor": jnp.clip(1.0 + 0.18 * jax.random.normal(keys[7], (SKY_LAYERS,), jnp.float32), 0.1, 1.9),
        "marine_heat_matrix": centred(keys[8], (MARINE_QUANTITY, SKY_LAYERS), MARINE_QUANTITY ** -0.5, 2.0, (), jnp.float32),
        "sky_expansion_matrix": centred(keys[9], (SKY_LAYERS, HA), SKY_LAYERS ** -0.5, 0.25),
        "sky_projection_matrix": centred(keys[10], (HA, SKY_LAYERS), HA ** -0.5, 0.1875),
        "exchange_output_matrix": centred(keys[11], (SKY_LAYERS, NF), SKY_LAYERS ** -0.5, 0.25),
        "marine_stencil_filter": centred(keys[12], (9, CO), 0.33, 2.0, (), jnp.float32),
        "marine_scale_factor": jnp.clip(1.0 + 0.18 * jax.random.normal(keys[13], (CO,), jnp.float32), 0.1, 1.9),
        "exchange_into_marine_matrix": centred(keys[14], (NF, CO), NF ** -0.5, 1.5, (), jnp.float32),
        "marine_expansion_matrix": centred(keys[15], (CO, HO), CO ** -0.5, 0.375),
        "marine_projection_matrix": centred(keys[16], (HO, CO), HO ** -0.5, 0.25),
        "marine_interface_matrix": centred(keys[17], (CO, MARINE_QUANTITY), CO ** -0.5, 0.375),
    }


def rotate(values, code):
    half = values.shape[-1] // 2
    first = values[..., :half]
    second = values[..., half:]
    cosine = (code == 0).astype(jnp.float32) - (code == 2).astype(jnp.float32)
    sine = (code == 1).astype(jnp.float32) - (code == 3).astype(jnp.float32)
    return jnp.concatenate([cosine * first - sine * second, sine * first + cosine * second], axis=-1)

def normalize(values, scale_factor):
    centre = lax.optimization_barrier(jnp.mean(values, axis=-1, keepdims=True))
    shifted_vals = values - centre
    spread = lax.optimization_barrier(jnp.mean(shifted_vals * shifted_vals, axis=-1, keepdims=True))
    return shifted_vals * lax.rsqrt(spread + 1e-05) * scale_factor

def pooled(values):
    shape = values.shape
    grouped = values.reshape(shape[0], shape[1] // 2, 2, shape[2] // 2, 2, shape[3])
    return lax.optimization_barrier(jnp.sum(grouped, axis=(2, 4)))

def sky_delta(sky_quantity, band_line_entries, pooled_marine_heat, stencil_filter, scale_factor, marine_heat_matrix, expansion_matrix, projection_matrix):
    accumulated_sum = jnp.einsum('lved,dp->lvep', pooled_marine_heat, marine_heat_matrix, precision=lax.Precision.HIGHEST)
    for row_off in range(3):
        for col_off in range(3):
            accumulated_sum = accumulated_sum + stencil_filter[3 * row_off + col_off] * jnp.roll(band_line_entries[row_off], 1 - col_off, axis=2)
    width = sky_quantity.shape[-1]
    normed = normalize(accumulated_sum, scale_factor).astype(jnp.bfloat16).reshape(-1, width)
    hidden = jax.nn.gelu(jnp.dot(normed, expansion_matrix, preferred_element_type=jnp.float32), approximate=True).astype(jnp.bfloat16)
    update = jnp.dot(hidden, projection_matrix, preferred_element_type=jnp.float32).reshape(sky_quantity.shape)
    return (sky_quantity.astype(jnp.float32) + update).astype(jnp.bfloat16)

def sea_update(marine_quantity, shifted, forcing_in, marine_indicator_real, stencil_filter, scale_factor, exchange_into_marine_matrix, expansion_matrix, projection_matrix):
    accumulated_sum = jnp.einsum('brcf,fk->brck', forcing_in, exchange_into_marine_matrix, precision=lax.Precision.HIGHEST)
    for row_off in range(3):
        for col_off in range(3):
            accumulated_sum = accumulated_sum + stencil_filter[3 * row_off + col_off] * shifted(row_off, col_off)
    width = marine_quantity.shape[-1]
    normed = normalize(accumulated_sum, scale_factor).astype(jnp.bfloat16).reshape(-1, width)
    hidden = jax.nn.gelu(jnp.dot(normed, expansion_matrix, preferred_element_type=jnp.float32), approximate=True).astype(jnp.bfloat16)
    update = jnp.dot(hidden, projection_matrix, preferred_element_type=jnp.float32).reshape(marine_quantity.shape)
    return (marine_quantity.astype(jnp.float32) + marine_indicator_real[None, :, :, None] * update).astype(jnp.bfloat16)

def interface_heats(marine_quantity, marine_indicator_real, marine_interface_matrix, grid_pixel_number):
    shape = marine_quantity.shape
    fine = jnp.dot(marine_quantity.reshape(-1, shape[3]), marine_interface_matrix, preferred_element_type=jnp.float32)
    fine = fine.astype(jnp.bfloat16).reshape(shape[0], shape[1], shape[2], -1)
    masked = fine.astype(jnp.float32) * marine_indicator_real[None, :, :, None]
    return pooled(masked) / jnp.maximum(grid_pixel_number, 1.0)

def reference(sky_velocity_tensor, marine_tensor, above_rotation_quarters, beneath_rotation_quarters, covering_pixels, marine_pixel_indicator, sky_stencil_filter, sky_scale_factor, marine_heat_matrix, sky_expansion_matrix, sky_projection_matrix, exchange_output_matrix, marine_stencil_filter, marine_scale_factor, exchange_into_marine_matrix, marine_expansion_matrix, marine_projection_matrix, marine_interface_matrix):
    marine_indicator_real = marine_pixel_indicator.astype(jnp.float32)
    grid_pixel_number = pooled(marine_indicator_real[None, :, :, None])
    rows_grid = jnp.arange(OROWS).astype(jnp.int32)[:, None, None]
    cols_grid = jnp.arange(OCOLS).astype(jnp.int32)[None, :, None]
    air_row = rows_grid // ORD * ABR + covering_pixels // ABC
    air_col = cols_grid // OCD * ABC + covering_pixels % ABC
    flat_index = (air_row * AC + air_col).reshape(-1).astype(jnp.int32)
    codes_upper = above_rotation_quarters[None, :, None, None]
    codes_lower = beneath_rotation_quarters[None, :, None, None]
    sky_quantity = sky_velocity_tensor
    marine_quantity = marine_tensor
    for step in range(NSTEP):
        pooled_marine_heat = interface_heats(marine_quantity, marine_indicator_real, marine_interface_matrix, grid_pixel_number)
        centre_adjacent = sky_quantity.astype(jnp.float32)
        above_adjacent = rotate(jnp.roll(centre_adjacent, 1, axis=1), codes_upper)
        beneath_adjacent = rotate(jnp.roll(centre_adjacent, -1, axis=1), codes_lower)
        sky_quantity = sky_delta(sky_quantity, (above_adjacent, centre_adjacent, beneath_adjacent), pooled_marine_heat, sky_stencil_filter, sky_scale_factor, marine_heat_matrix, sky_expansion_matrix, sky_projection_matrix)
        flux = jnp.dot(sky_quantity.reshape(-1, SKY_LAYERS), exchange_output_matrix, preferred_element_type=jnp.float32).astype(jnp.bfloat16)
        flux = flux.reshape(B, AROWS * AC, NF)
        picked = jnp.take(flux, flat_index, axis=1).astype(jnp.float32).reshape(B, OROWS, OCOLS, K, NF)
        forcing_in = lax.optimization_barrier(jnp.mean(picked, axis=3))
        ocean_f = marine_quantity.astype(jnp.float32)

        def shifted(row_off, col_off, ocean_f=ocean_f):
            return jnp.roll(jnp.roll(ocean_f, 1 - row_off, axis=1), 1 - col_off, axis=2)
        marine_quantity = sea_update(marine_quantity, shifted, forcing_in, marine_indicator_real, marine_stencil_filter, marine_scale_factor, exchange_into_marine_matrix, marine_expansion_matrix, marine_projection_matrix)
    return (sky_quantity, marine_quantity)
```

```python
import functools

import jax
import jax.numpy as jnp
from jax import lax
from jax.experimental import pallas as pl
from jax.experimental.pallas import tpu as pltpu
from jax.sharding import PartitionSpec as P

MESH = pl.DeviceIdType.MESH
F32 = jnp.float32
BF16 = jnp.bfloat16
NSTEP = 2
SIDES = [(-1, 0), (1, 0), (0, -1), (0, 1), (-1, -1), (-1, 1), (1, -1), (1, 1)]


def gelu(x):
    inner = x * (0.7978845608028654 + 0.035677408136300125 * (x * x))
    half = 0.5 * x
    return half + half * jnp.tanh(inner)


def normed(z, gain):
    shifted = z - jnp.mean(z, axis=-1, keepdims=True)
    spread = jnp.mean(shifted * shifted, axis=-1, keepdims=True)
    return (shifted * lax.rsqrt(spread + 1e-05) * gain).astype(BF16)


def spread_over_lanes(rows, lanes):
    r = lax.broadcasted_iota(jnp.int32, (rows, lanes), 0)
    c = lax.broadcasted_iota(jnp.int32, (rows, lanes), 1)
    return (lax.rem(c, rows) == r).astype(BF16)


def kernel(
    na, no,
    above, beneath, cover, sea_flag,
    sky, sea, sky_filter, sky_gain, heat, sky_in, sky_back, to_flux, sea_filter, sea_gain, from_flux, sea_in, sea_back, to_sst,
    sky_out, sea_out,
    raw_sky, raw_sea, v_sky_filter, v_sky_gain, v_heat, v_sky_in, v_sky_back, v_to_flux, v_sea_filter, v_sea_gain, v_from_flux,
    v_sea_in, v_sea_back, v_to_sst,
    tok_sky, tok_sea, air, up, down, ocean, ext, zbuf, ubuf, hbuf,
    flux_wide, heat_wide, into_wide, sst_wide, cellw, seaw, poolw,
    sst_tx, sst_rx, flux_tx, flux_rx,
    in_sem, sst_send, sst_recv, flux_send, flux_recv, self_sem, air_send, air_recv, sea_send, sea_recv, out_sem,
):
    a = lax.axis_index("atm")
    o = lax.axis_index("ocn")
    half_a = a // 2
    mine = half_a == o

    def at(atm, ocn):
        return {"atm": lax.rem(atm + na, na), "ocn": lax.rem(ocn + no, no)}

    def is_me(atm, ocn):
        return jnp.logical_and(atm == a, ocn == o)

    barrier = pltpu.get_barrier_semaphore()

    def greet_a(k, c):
        for rr in range(2):
            @pl.when(jnp.logical_not(is_me(2 * o + rr, k)))
            def _():
                pl.semaphore_signal(barrier, inc=1, device_id=at(2 * o + rr, k), device_id_type=MESH)
        return c

    def greet_b(q, c):
        @pl.when(jnp.logical_not(is_me(q, half_a)))
        def _():
            pl.semaphore_signal(barrier, inc=1, device_id=at(q, half_a), device_id_type=MESH)
        return c

    lax.fori_loop(0, no, greet_a, 0)
    lax.fori_loop(0, na, greet_b, 0)
    for di, dj in SIDES:
        pl.semaphore_signal(barrier, inc=1, device_id=at(a + dj, o + di), device_id_type=MESH)

    loads = [
        pltpu.make_async_copy(src, dst, in_sem.at[n])
        for n, (src, dst) in enumerate([
            (sea, raw_sea), (sky, raw_sky), (to_sst, v_to_sst), (sky_filter, v_sky_filter), (heat, v_heat),
            (sky_gain, v_sky_gain), (sky_in, v_sky_in), (sky_back, v_sky_back), (to_flux, v_to_flux),
            (sea_filter, v_sea_filter), (sea_gain, v_sea_gain), (from_flux, v_from_flux), (sea_in, v_sea_in),
            (sea_back, v_sea_back),
        ])
    ]
    for load in loads:
        load.start()

    lane = lax.broadcasted_iota(jnp.int32, (no, 128), 1)

    def tables(cell, c):
        row, col = cell // 8, lax.rem(cell, 8)
        flag = jnp.full((no, 256), sea_flag[row, col], jnp.int32).astype(F32)
        r0, c0 = row // 2 * 2, col // 2 * 2
        count = sea_flag[r0, c0] + sea_flag[r0, c0 + 1] + sea_flag[r0 + 1, c0] + sea_flag[r0 + 1, c0 + 1]
        count = jnp.full((no, 256), count, jnp.int32).astype(F32)
        seaw[cell] = flag
        poolw[cell] = flag / jnp.maximum(count, 1.0)
        share = jnp.zeros((no, 128), F32)
        for k in range(4):
            share = share + jnp.where(lane // 16 == cover[row, k, col], 0.25, 0.0)
        cellw[cell] = share
        return c

    lax.fori_loop(0, 32, tables, 0)

    loads[0].wait()
    per = 2 * no // 4

    def open_sea(n, c):
        part = raw_sea[pl.ds(n * per, per)].astype(F32)
        part = part.reshape(per * 32, 256)
        for w in range(2):
            tok_sea[w, pl.ds(pl.multiple_of(n * per * 32, per * 32), per * 32), :] = part[:, 128 * w : 128 * w + 128]
        return c

    lax.fori_loop(0, 4, open_sea, 0)

    def sort_sea(cell, c):
        row, col = cell // 8, lax.rem(cell, 8)
        for par in range(2):
            for w in range(2):
                part = tok_sea[w, pl.ds(par * 32 + cell, no, stride=64), :]
                ocean[0, par, 1 + row, 1 + col, :, 128 * w : 128 * w + 128] = part.astype(BF16)
        return c

    lax.fori_loop(0, 32, sort_sea, 0)

    loads[1].wait()
    for w in range(4):
        tok_sky[w] = raw_sky[:, :, :, 128 * w : 128 * w + 128].astype(F32).reshape(8 * na, 128)

    def sort_sky(cc, c):
        for par in range(2):
            for w in range(4):
                part = tok_sky[w, pl.ds(par * 4 * na + cc, na, stride=4), :]
                air[0, par, cc, :, 128 * w : 128 * w + 128] = part.astype(BF16)
        return c

    lax.fori_loop(0, 4, sort_sky, 0)

    loads[2].wait()
    sst_wide[...] = lax.dot_general(
        v_to_sst[...], spread_over_lanes(8, 128), (((0,), (0,)), ((), ())), preferred_element_type=F32
    ).astype(BF16)

    def put_air(step, par):
        return [
            pltpu.make_async_remote_copy(
                src_ref=air.at[step, par], dst_ref=there.at[step, par], send_sem=air_send.at[step, par, n],
                recv_sem=air_recv.at[step, par, n], device_id=at(a + da, o), device_id_type=MESH,
            )
            for n, (there, da) in enumerate([(up, 1), (down, -1)])
        ]

    def put_sea(step, par):
        copies = []
        for n, (di, dj) in enumerate(SIDES):
            rows = {-1: 1, 0: pl.ds(1, 4), 1: 4}[di]
            cols = {-1: 1, 0: pl.ds(1, 8), 1: 8}[dj]
            to_rows = {-1: 5, 0: pl.ds(1, 4), 1: 0}[di]
            to_cols = {-1: 9, 0: pl.ds(1, 8), 1: 0}[dj]
            copies.append(
                pltpu.make_async_remote_copy(
                    src_ref=ocean.at[step, par, rows, cols], dst_ref=ocean.at[step, par, to_rows, to_cols],
                    send_sem=sea_send.at[step, par, n], recv_sem=sea_recv.at[step, par, n],
                    device_id=at(a + dj, o + di), device_id_type=MESH,
                )
            )
        return copies

    def start(copies):
        for copy in copies:
            copy.start()

    def send_sst(step, par):
        def block_rows(rr, c):
            parts = []
            for cc in range(4):
                sums = jnp.zeros((no, 256), F32)
                for i in range(2):
                    for j in range(2):
                        cell = (2 * rr + i) * 8 + 2 * cc + j
                        sums = sums + poolw[cell] * ocean[step, par, 1 + 2 * rr + i, 1 + 2 * cc + j].astype(F32)
                parts.append(sums.astype(BF16))
            lines = jnp.zeros((no, 128), F32)
            which = lax.rem(lane // 8, 4)
            for cc in range(4):
                got = jnp.dot(parts[cc], sst_wide[...], preferred_element_type=F32)
                lines = jnp.where(which == cc, got, lines)
            sst_tx[step, par, pl.ds(rr * no, no)] = lines.reshape(no, 1, 128)
            return c

        lax.fori_loop(0, 2, block_rows, 0)

        def put(k, c):
            for rr in range(2):
                src = sst_tx.at[step, par, rr * no + k]
                dst = sst_rx.at[step, par, a]
                there = is_me(2 * o + rr, k)

                @pl.when(jnp.logical_not(there))
                def _():
                    pltpu.make_async_remote_copy(
                        src_ref=src, dst_ref=dst, send_sem=sst_send.at[step, par], recv_sem=sst_recv.at[step, par],
                        device_id=at(2 * o + rr, k), device_id_type=MESH,
                    ).start()

                @pl.when(there)
                def _():
                    pltpu.make_async_copy(src, dst, self_sem.at[step, par, 0]).start()
            return c

        lax.fori_loop(0, no, put, 0)

    def send_flux(step, par):
        def put(q, c):
            src = flux_tx.at[step, par, q]
            dst = flux_rx.at[step, par, lax.rem(a, 2) * no + o]
            there = is_me(q, half_a)

            @pl.when(jnp.logical_not(there))
            def _():
                pltpu.make_async_remote_copy(
                    src_ref=src, dst_ref=dst, send_sem=flux_send.at[step, par], recv_sem=flux_recv.at[step, par],
                    device_id=at(q, half_a), device_id_type=MESH,
                ).start()

            @pl.when(there)
            def _():
                pltpu.make_async_copy(src, dst, self_sem.at[step, par, 1]).start()
            return c

        lax.fori_loop(0, na, put, 0)

    def rows_of(buf, sem_send, sem_recv, step, par, count):
        part = buf.at[step, par, pl.ds(0, count)]
        return pltpu.make_async_remote_copy(
            src_ref=part, dst_ref=part, send_sem=sem_send.at[step, par], recv_sem=sem_recv.at[step, par],
            device_id=at(a, o), device_id_type=MESH,
        )

    def exchange_wait(buf, sem_send, sem_recv, step, par, n, received):
        @pl.when(mine)
        def _():
            copy = rows_of(buf, sem_send, sem_recv, step, par, na - 1)
            if received:
                pltpu.make_async_copy(buf.at[step, par, 0], buf.at[step, par, 0], self_sem.at[step, par, n]).wait()
                copy.wait_recv()
            else:
                copy.wait_send()

        @pl.when(jnp.logical_not(mine))
        def _():
            copy = rows_of(buf, sem_send, sem_recv, step, par, na)
            if received:
                copy.wait_recv()
            else:
                copy.wait_send()


    @pl.when(mine)
    def _():
        pl.semaphore_wait(barrier, 2 * na + 6)

    @pl.when(jnp.logical_not(mine))
    def _():
        pl.semaphore_wait(barrier, 2 * na + 8)

    for par in range(2):
        start(put_air(0, par))
    for par in range(2):
        send_sst(0, par)
    for par in range(2):
        start(put_sea(0, par))

    for load in loads[3:]:
        load.wait()
    flux_wide[...] = lax.dot_general(
        v_to_flux[...], spread_over_lanes(16, 128), (((0,), (0,)), ((), ())), preferred_element_type=F32
    ).astype(BF16)
    heat_wide[...] = lax.dot_general(
        spread_over_lanes(8, 128), v_heat[...].astype(BF16), (((0,), (0,)), ((), ())), preferred_element_type=F32
    ).astype(BF16)
    into_wide[...] = lax.dot_general(
        spread_over_lanes(16, 128), v_from_flux[...].astype(BF16), (((0,), (0,)), ((), ())), preferred_element_type=F32
    ).astype(BF16)

    turns = []
    for code in (above[0], beneath[0]):
        cosine = jnp.where(code == 0, 1.0, 0.0) - jnp.where(code == 2, 1.0, 0.0)
        sine = jnp.where(code == 1, 1.0, 0.0) - jnp.where(code == 3, 1.0, 0.0)
        turns.append((cosine, sine))

    lane_a = lax.broadcasted_iota(jnp.int32, (na, 128), 1)

    def sky_part(step, par):
        for copy in put_air(step, par):
            copy.wait_recv()

        def frame(cc, c):
            ext[1, cc + 1] = air[step, par, cc].astype(F32)
            for n, src in ((0, up), (2, down)):
                cosine, sine = turns[n // 2]
                east = src[step, par, cc, :, :256].astype(F32)
                north = src[step, par, cc, :, 256:].astype(F32)
                ext[n, cc + 1, :, :256] = cosine * east - sine * north
                ext[n, cc + 1, :, 256:] = sine * east + cosine * north
            return c

        lax.fori_loop(0, 4, frame, 0)

        def ends(n, c):
            ext[n, 0] = pltpu.roll(ext[n, 4], 1, 0)
            ext[n, 5] = pltpu.roll(ext[n, 1], na - 1, 0)
            return c

        lax.fori_loop(0, 3, ends, 0)

        exchange_wait(sst_rx, sst_send, sst_recv, step, par, 0, True)
        fields = sst_rx[step, par].reshape(na, 128)
        for cc in range(4):
            one = jnp.where(lane_a // 8 == cc, fields, 0.0).astype(BF16)
            zbuf[cc] = jnp.dot(one, heat_wide[...], preferred_element_type=F32)

        def column(cc, c):
            z = zbuf[cc]
            for i in range(3):
                for j in range(3):
                    z = z + v_sky_filter[3 * i + j : 3 * i + j + 1, :] * ext[i, cc + j]
            ubuf[cc] = normed(z, v_sky_gain[...])
            return c

        lax.fori_loop(0, 4, column, 0)
        u = ubuf[...].reshape(4 * na, 512)
        for n in range(4):
            part = slice(256 * n, 256 * n + 256)
            hbuf[:, part] = gelu(jnp.dot(u, v_sky_in[:, part], preferred_element_type=F32)).astype(BF16)
        for n in range(2):
            part = slice(256 * n, 256 * n + 256)
            change = jnp.dot(hbuf[...], v_sky_back[:, part], preferred_element_type=F32)
            old = air[step, par, :, :, part].astype(F32)
            air[step + 1, par, :, :, part] = (old + change.reshape(4, na, 256)).astype(BF16)
        lines = jnp.zeros((na, 128), F32)
        for cc in range(4):
            got = jnp.dot(air[step + 1, par, cc], flux_wide[...], preferred_element_type=F32)
            lines = jnp.where(lax.rem(lane_a // 16, 4) == cc, got, lines)
        flux_tx[step, par] = lines.reshape(na, 1, 128)
        send_flux(step, par)

        @pl.when(step + 1 < NSTEP)
        def _():
            start(put_air(step + 1, par))

        @pl.when(step + 1 == NSTEP)
        def _():
            pltpu.make_async_copy(air.at[step + 1, par], sky_out.at[par], out_sem.at[par]).start()

    def sea_part(step, par):
        for copy in put_sea(step, par):
            copy.wait_recv()
        exchange_wait(flux_rx, flux_send, flux_recv, step, par, 1, True)
        got = flux_rx[step, par].reshape(2 * no, 128)
        fields = jnp.where(lane < 64, got[:no], got[no:])

        def line(row, c):
            cells = pl.ds(pl.multiple_of(row * 8, 8), 8)
            lhs = (cellw[cells] * fields[None]).astype(BF16).reshape(8 * no, 128)
            z = jnp.dot(lhs, into_wide[...], preferred_element_type=F32).reshape(8, no, 256)
            for i in range(3):
                for j in range(3):
                    tap = v_sea_filter[3 * i + j : 3 * i + j + 1, :]
                    z = z + tap[None] * ocean[step, par, row + i, j : j + 8].astype(F32)
            u = normed(z.reshape(8 * no, 256), v_sea_gain[...])
            hidden = gelu(jnp.dot(u, v_sea_in[...], preferred_element_type=F32)).astype(BF16)
            change = jnp.dot(hidden, v_sea_back[...], preferred_element_type=F32).reshape(8, no, 256)
            old = ocean[step, par, row + 1, 1:9].astype(F32)
            ocean[step + 1, par, row + 1, 1:9] = (old + seaw[cells] * change).astype(BF16)
            return c

        lax.fori_loop(0, 4, line, 0)

        @pl.when(step + 1 < NSTEP)
        def _():
            send_sst(step + 1, par)
            start(put_sea(step + 1, par))

        @pl.when(step + 1 == NSTEP)
        def _():
            pltpu.make_async_copy(
                ocean.at[step + 1, par, pl.ds(1, 4), pl.ds(1, 8)], sea_out.at[par], out_sem.at[2 + par]
            ).start()

    def one_step(step, c):
        def sky_loop(par, c):
            sky_part(step, par)
            return c

        def sea_loop(par, c):
            sea_part(step, par)
            return c

        lax.fori_loop(0, 2, sky_loop, 0)
        lax.fori_loop(0, 2, sea_loop, 0)
        return c

    lax.fori_loop(0, NSTEP, one_step, 0)

    def close(n, c):
        step, par = n // 2, lax.rem(n, 2)
        for copy in put_air(step, par) + put_sea(step, par):
            copy.wait_send()
        exchange_wait(sst_tx, sst_send, sst_recv, step, par, 0, False)
        exchange_wait(flux_tx, flux_send, flux_recv, step, par, 1, False)
        return c

    lax.fori_loop(0, 2 * NSTEP, close, 0)
    for par in range(2):
        pltpu.make_async_copy(air.at[NSTEP, par], sky_out.at[par], out_sem.at[par]).wait()
        pltpu.make_async_copy(
            ocean.at[NSTEP, par, pl.ds(1, 4), pl.ds(1, 8)], sea_out.at[par], out_sem.at[2 + par]
        ).wait()


def local(na, no, sky, sea, above, beneath, cover, sea_flag, sky_filter, sky_gain, heat, sky_in, sky_back, to_flux,
          sea_filter, sea_gain, from_flux, sea_in, sea_back, to_sst):
    smem = pl.BlockSpec(memory_space=pltpu.SMEM)
    hbm = pl.BlockSpec(memory_space=pl.ANY)
    vmem = pltpu.VMEM
    dma = pltpu.SemaphoreType.DMA
    n, p = NSTEP, 2
    big = [sky, sea, sky_filter, sky_gain[None], heat, sky_in, sky_back, to_flux.T, sea_filter, sea_gain[None], from_flux, sea_in,
           sea_back, to_sst.T]
    sky_new, sea_new = pl.pallas_call(
        functools.partial(kernel, na, no),
        out_shape=(
            jax.ShapeDtypeStruct((p, 4, na, 512), BF16),
            jax.ShapeDtypeStruct((p, 4, 8, no, 256), BF16),
        ),
        in_specs=[smem] * 4 + [hbm] * len(big),
        out_specs=(hbm, hbm),
        scratch_shapes=[vmem(x.shape, x.dtype) for x in big] + [
            vmem((4, p * 4 * na, 128), F32),
            vmem((2, 2 * no * 32, 128), F32),
            vmem((n + 1, p, 4, na, 512), BF16),
            vmem((n, p, 4, na, 512), BF16),
            vmem((n, p, 4, na, 512), BF16),
            vmem((n + 1, p, 6, 10, no, 256), BF16),
            vmem((3, 6, na, 512), F32),
            vmem((4, na, 512), F32),
            vmem((4, na, 512), BF16),
            vmem((4 * na, 1024), BF16),
            vmem((512, 128), BF16),
            vmem((128, 512), BF16),
            vmem((128, 256), BF16),
            vmem((256, 128), BF16),
            vmem((32, no, 128), F32),
            vmem((32, no, 256), F32),
            vmem((32, no, 256), F32),
            vmem((n, p, na, 1, 128), F32),
            vmem((n, p, na, 1, 128), F32),
            vmem((n, p, na, 1, 128), F32),
            vmem((n, p, na, 1, 128), F32),
            dma((len(big),)),
            dma((n, p)),
            dma((n, p)),
            dma((n, p)),
            dma((n, p)),
            dma((n, p, 2)),
            dma((n, p, 2)),
            dma((n, p, 2)),
            dma((n, p, 8)),
            dma((n, p, 8)),
            dma((4,)),
        ],
        compiler_params=pltpu.CompilerParams(
            collective_id=0, has_side_effects=True, vmem_limit_bytes=56 * 1024 * 1024
        ),
        name="coupled_steps",
    )(above, beneath, cover.transpose(0, 2, 1), sea_flag, *big)
    sky_new = sky_new.transpose(0, 2, 1, 3).reshape(sky.shape)
    sea_new = sea_new.transpose(3, 0, 1, 2, 4).reshape(sea.shape)
    return sky_new, sea_new


def solution(mesh):
    return jax.shard_map(
        functools.partial(local, mesh.shape["atm"], mesh.shape["ocn"]),
        mesh=mesh,
        in_specs=(
            P("ocn", "atm", None, None),
            P(None, "ocn", "atm", None),
            P("atm"),
            P("atm"),
            P("ocn", "atm", None),
            P("ocn", "atm"),
        ) + (P(),) * 12,
        out_specs=(P("ocn", "atm", None, None), P(None, "ocn", "atm", None)),
        check_vma=False,
    )
```

```python
import functools

import jax
import jax.numpy as jnp
from jax import lax
from jax.experimental import pallas as pl
from jax.experimental.pallas import tpu as pltpu
from jax.sharding import PartitionSpec as P

MESH = pl.DeviceIdType.MESH
F32 = jnp.float32
BF16 = jnp.bfloat16
NSTEP = 2
SIDES = [(-1, 0), (1, 0), (0, -1), (0, 1), (-1, -1), (-1, 1), (1, -1), (1, 1)]


def gelu(x):
    inner = x * (0.7978845608028654 + 0.035677408136300125 * (x * x))
    half = 0.5 * x
    return half + half * jnp.tanh(inner)


def normed(z, gain):
    shifted = z - jnp.mean(z, axis=-1, keepdims=True)
    spread = jnp.mean(shifted * shifted, axis=-1, keepdims=True)
    return (shifted * lax.rsqrt(spread + 1e-05) * gain).astype(BF16)


def spread_over_lanes(rows, lanes):
    r = lax.broadcasted_iota(jnp.int32, (rows, lanes), 0)
    c = lax.broadcasted_iota(jnp.int32, (rows, lanes), 1)
    return (lax.rem(c, rows) == r).astype(BF16)


def kernel(
    na, no,
    above, beneath, cover, sea_flag,
    sky, sea, sky_filter, sky_gain, heat, sky_in, sky_back, to_flux, sea_filter, sea_gain, from_flux, sea_in, sea_back, to_sst,
    sky_out, sea_out,
    raw_sky, raw_sea, v_sky_filter, v_sky_gain, v_heat, v_sky_in, v_sky_back, v_to_flux, v_sea_filter, v_sea_gain, v_from_flux,
    v_sea_in, v_sea_back, v_to_sst,
    tok_sky, tok_sea, air, up, down, ocean, ext, zbuf, ubuf, hbuf,
    flux_wide, heat_wide, into_wide, sst_wide, cellw, seaw, poolw,
    sst_tx, sst_rx, flux_tx, flux_rx,
    in_sem, sst_send, sst_recv, flux_send, flux_recv, self_sem, air_send, air_recv, sea_send, sea_recv, out_sem,
):
    a = lax.axis_index("atm")
    o = lax.axis_index("ocn")
    half_a = a // 2
    mine = half_a == o

    def at(atm, ocn):
        return {"atm": lax.rem(atm + na, na), "ocn": lax.rem(ocn + no, no)}

    def is_me(atm, ocn):
        return jnp.logical_and(atm == a, ocn == o)

    loads = [
        pltpu.make_async_copy(src, dst, in_sem.at[n])
        for n, (src, dst) in enumerate([
            (sea, raw_sea), (sky, raw_sky), (to_sst, v_to_sst), (sky_filter, v_sky_filter), (heat, v_heat),
            (sky_gain, v_sky_gain), (sky_in, v_sky_in), (sky_back, v_sky_back), (to_flux, v_to_flux),
            (sea_filter, v_sea_filter), (sea_gain, v_sea_gain), (from_flux, v_from_flux), (sea_in, v_sea_in),
            (sea_back, v_sea_back),
        ])
    ]
    for load in loads:
        load.start()

    barrier = pltpu.get_barrier_semaphore()

    def greet(n, c):
        pl.semaphore_signal(barrier, inc=1, device_id=at(a + n, half_a), device_id_type=MESH)
        return c

    lax.fori_loop(1, na, greet, 0)

    @pl.when(jnp.logical_not(mine))
    def _():
        pl.semaphore_signal(barrier, inc=1, device_id=at(a, half_a), device_id_type=MESH)

    for di, dj in SIDES:
        pl.semaphore_signal(barrier, inc=1, device_id=at(a + dj, o + di), device_id_type=MESH)

    lane = lax.broadcasted_iota(jnp.int32, (no, 128), 1)

    def pool_table(cell, c):
        row, col = cell // 8, lax.rem(cell, 8)
        flag = jnp.full((no, 256), sea_flag[row, col], jnp.int32).astype(F32)
        r0, c0 = row // 2 * 2, col // 2 * 2
        count = sea_flag[r0, c0] + sea_flag[r0, c0 + 1] + sea_flag[r0 + 1, c0] + sea_flag[r0 + 1, c0 + 1]
        count = jnp.full((no, 256), count, jnp.int32).astype(F32)
        seaw[cell] = flag
        poolw[cell] = flag / jnp.maximum(count, 1.0)
        return c

    lax.fori_loop(0, 32, pool_table, 0)

    def cell_table(cell, c):
        row, col = cell // 8, lax.rem(cell, 8)
        share = jnp.zeros((no, 128), F32)
        for k in range(4):
            share = share + jnp.where(lane // 16 == cover[row, k, col], 0.25, 0.0)
        cellw[cell] = share
        return c

    loads[0].wait()
    per = 2 * no // 4

    def open_sea(n, c):
        part = raw_sea[pl.ds(n * per, per)].astype(F32)
        part = part.reshape(per * 32, 256)
        for w in range(2):
            tok_sea[w, pl.ds(pl.multiple_of(n * per * 32, per * 32), per * 32), :] = part[:, 128 * w : 128 * w + 128]
        return c

    lax.fori_loop(0, 4, open_sea, 0)

    def sort_sea(par):
        def sort_cell(cell, c):
            row, col = cell // 8, lax.rem(cell, 8)
            for w in range(2):
                part = tok_sea[w, pl.ds(par * 32 + cell, no, stride=64), :]
                ocean[0, par, 1 + row, 1 + col, :, 128 * w : 128 * w + 128] = part.astype(BF16)
            return c

        lax.fori_loop(0, 32, sort_cell, 0)

    loads[2].wait()
    sst_wide[...] = lax.dot_general(
        v_to_sst[...], spread_over_lanes(8, 128), (((0,), (0,)), ((), ())), preferred_element_type=F32
    ).astype(BF16)

    def put_air(step, par):
        return [
            pltpu.make_async_remote_copy(
                src_ref=air.at[step, par], dst_ref=there.at[step, par], send_sem=air_send.at[step, par, n],
                recv_sem=air_recv.at[step, par, n], device_id=at(a + da, o), device_id_type=MESH,
            )
            for n, (there, da) in enumerate([(up, 1), (down, -1)])
        ]

    def put_sea(step, par):
        copies = []
        for n, (di, dj) in enumerate(SIDES):
            rows = {-1: 1, 0: pl.ds(1, 4), 1: 4}[di]
            cols = {-1: 1, 0: pl.ds(1, 8), 1: 8}[dj]
            to_rows = {-1: 5, 0: pl.ds(1, 4), 1: 0}[di]
            to_cols = {-1: 9, 0: pl.ds(1, 8), 1: 0}[dj]
            copies.append(
                pltpu.make_async_remote_copy(
                    src_ref=ocean.at[step, par, rows, cols], dst_ref=ocean.at[step, par, to_rows, to_cols],
                    send_sem=sea_send.at[step, par, n], recv_sem=sea_recv.at[step, par, n],
                    device_id=at(a + dj, o + di), device_id_type=MESH,
                )
            )
        return copies

    def start(copies):
        for copy in copies:
            copy.start()

    def make_sst(step, par):
        def block_rows(rr, c):
            parts = []
            for cc in range(4):
                sums = jnp.zeros((no, 256), F32)
                for i in range(2):
                    for j in range(2):
                        cell = (2 * rr + i) * 8 + 2 * cc + j
                        sums = sums + poolw[cell] * ocean[step, par, 1 + 2 * rr + i, 1 + 2 * cc + j].astype(F32)
                parts.append(sums.astype(BF16))
            lines = jnp.zeros((no, 128), F32)
            which = lax.rem(lane // 8, 4)
            for cc in range(4):
                got = jnp.dot(parts[cc], sst_wide[...], preferred_element_type=F32)
                lines = jnp.where(which == cc, got, lines)
            sst_tx[step, par, pl.ds(rr * no, no)] = lines.reshape(no, 1, 128)
            return c

        lax.fori_loop(0, 2, block_rows, 0)

    def send_sst(step, par):
        def put(ocn, rr):
            return pltpu.make_async_remote_copy(
                src_ref=sst_tx.at[step, par, rr * no + ocn], dst_ref=sst_rx.at[step, par, a],
                send_sem=sst_send.at[step, par], recv_sem=sst_recv.at[step, par],
                device_id=at(2 * o + rr, ocn), device_id_type=MESH,
            )

        apart = min(4, no)
        for d in sorted(range(apart), key=lambda d: -min(d, apart - d)):
            def put_group(y, c, d=d):
                ocn = y * apart + lax.rem(o + d, apart)
                if d:
                    for rr in range(2):
                        put(ocn, rr).start()
                else:
                    for rr in range(2):
                        @pl.when(jnp.logical_not(is_me(2 * o + rr, ocn)))
                        def _():
                            put(ocn, rr).start()
                return c

            lax.fori_loop(0, no // apart, put_group, 0)

        @pl.when(mine)
        def _():
            pltpu.make_async_copy(
                sst_tx.at[step, par, lax.rem(a, 2) * no + o], sst_rx.at[step, par, a], self_sem.at[step, par, 0]
            ).start()

    def send_flux(step, par):
        place = lax.rem(a, 2) * no + o

        def put(atm):
            atm = lax.rem(atm + na, na)
            return pltpu.make_async_remote_copy(
                src_ref=flux_tx.at[step, par, atm], dst_ref=flux_rx.at[step, par, place],
                send_sem=flux_send.at[step, par], recv_sem=flux_recv.at[step, par],
                device_id=at(atm, half_a), device_id_type=MESH,
            )

        put(a + na // 2).start()

        def put_pair(n, c):
            put(a + na // 2 + n).start()
            put(a + na // 2 - n).start()
            return c

        lax.fori_loop(1, na // 2, put_pair, 0)

        @pl.when(jnp.logical_not(mine))
        def _():
            put(a).start()

        @pl.when(mine)
        def _():
            pltpu.make_async_copy(
                flux_tx.at[step, par, a], flux_rx.at[step, par, place], self_sem.at[step, par, 1]
            ).start()

    def rows_of(buf, sem_send, sem_recv, step, par, count):
        part = buf.at[step, par, pl.ds(0, count)]
        return pltpu.make_async_remote_copy(
            src_ref=part, dst_ref=part, send_sem=sem_send.at[step, par], recv_sem=sem_recv.at[step, par],
            device_id=at(a, o), device_id_type=MESH,
        )

    def exchange_wait(buf, sem_send, sem_recv, step, par, n, received):
        @pl.when(mine)
        def _():
            copy = rows_of(buf, sem_send, sem_recv, step, par, na - 1)
            if received:
                pltpu.make_async_copy(buf.at[step, par, 0], buf.at[step, par, 0], self_sem.at[step, par, n]).wait()
                copy.wait_recv()
            else:
                copy.wait_send()

        @pl.when(jnp.logical_not(mine))
        def _():
            copy = rows_of(buf, sem_send, sem_recv, step, par, na)
            if received:
                copy.wait_recv()
            else:
                copy.wait_send()


    sort_sea(0)
    make_sst(0, 0)

    @pl.when(mine)
    def _():
        pl.semaphore_wait(barrier, na + 7)

    @pl.when(jnp.logical_not(mine))
    def _():
        pl.semaphore_wait(barrier, na + 8)

    send_sst(0, 0)
    sort_sea(1)
    make_sst(0, 1)
    send_sst(0, 1)
    loads[1].wait()
    for w in range(4):
        tok_sky[w] = raw_sky[:, :, :, 128 * w : 128 * w + 128].astype(F32).reshape(8 * na, 128)

    def sort_sky(cc, c):
        for par in range(2):
            for w in range(4):
                part = tok_sky[w, pl.ds(par * 4 * na + cc, na, stride=4), :]
                air[0, par, cc, :, 128 * w : 128 * w + 128] = part.astype(BF16)
        return c

    lax.fori_loop(0, 4, sort_sky, 0)

    for par in range(2):
        start(put_air(0, par))
    start(put_sea(0, 0))

    lax.fori_loop(0, 32, cell_table, 0)

    for load in loads[3:]:
        load.wait()
    flux_wide[...] = lax.dot_general(
        v_to_flux[...], spread_over_lanes(16, 128), (((0,), (0,)), ((), ())), preferred_element_type=F32
    ).astype(BF16)
    heat_wide[...] = lax.dot_general(
        spread_over_lanes(8, 128), v_heat[...].astype(BF16), (((0,), (0,)), ((), ())), preferred_element_type=F32
    ).astype(BF16)
    into_wide[...] = lax.dot_general(
        spread_over_lanes(16, 128), v_from_flux[...].astype(BF16), (((0,), (0,)), ((), ())), preferred_element_type=F32
    ).astype(BF16)

    turns = []
    for code in (above[0], beneath[0]):
        cosine = jnp.where(code == 0, 1.0, 0.0) - jnp.where(code == 2, 1.0, 0.0)
        sine = jnp.where(code == 1, 1.0, 0.0) - jnp.where(code == 3, 1.0, 0.0)
        turns.append((cosine, sine))

    lane_a = lax.broadcasted_iota(jnp.int32, (na, 128), 1)

    def sky_part(step, par):
        for copy in put_air(step, par):
            copy.wait_recv()

        def frame(cc, c):
            ext[1, cc + 1] = air[step, par, cc].astype(F32)
            for n, src in ((0, up), (2, down)):
                cosine, sine = turns[n // 2]
                east = src[step, par, cc, :, :256].astype(F32)
                north = src[step, par, cc, :, 256:].astype(F32)
                ext[n, cc + 1, :, :256] = cosine * east - sine * north
                ext[n, cc + 1, :, 256:] = sine * east + cosine * north
            return c

        lax.fori_loop(0, 4, frame, 0)

        def ends(n, c):
            ext[n, 0] = pltpu.roll(ext[n, 4], 1, 0)
            ext[n, 5] = pltpu.roll(ext[n, 1], na - 1, 0)
            return c

        lax.fori_loop(0, 3, ends, 0)

        exchange_wait(sst_rx, sst_send, sst_recv, step, par, 0, True)
        fields = sst_rx[step, par].reshape(na, 128)
        for cc in range(4):
            one = jnp.where(lane_a // 8 == cc, fields, 0.0).astype(BF16)
            zbuf[cc] = jnp.dot(one, heat_wide[...], preferred_element_type=F32)

        def column(cc, c):
            z = zbuf[cc]
            for i in range(3):
                for j in range(3):
                    z = z + v_sky_filter[3 * i + j : 3 * i + j + 1, :] * ext[i, cc + j]
            ubuf[cc] = normed(z, v_sky_gain[...])
            return c

        lax.fori_loop(0, 4, column, 0)
        u = ubuf[...].reshape(4 * na, 512)
        for n in range(4):
            part = slice(256 * n, 256 * n + 256)
            hbuf[:, part] = gelu(jnp.dot(u, v_sky_in[:, part], preferred_element_type=F32)).astype(BF16)
        for n in range(2):
            part = slice(256 * n, 256 * n + 256)
            change = jnp.dot(hbuf[...], v_sky_back[:, part], preferred_element_type=F32)
            old = air[step, par, :, :, part].astype(F32)
            air[step + 1, par, :, :, part] = (old + change.reshape(4, na, 256)).astype(BF16)
        lines = jnp.zeros((na, 128), F32)
        for cc in range(4):
            got = jnp.dot(air[step + 1, par, cc], flux_wide[...], preferred_element_type=F32)
            lines = jnp.where(lax.rem(lane_a // 16, 4) == cc, got, lines)
        flux_tx[step, par] = lines.reshape(na, 1, 128)
        send_flux(step, par)

        @pl.when(step + 1 == NSTEP)
        def _():
            def unsort(cc, c):
                for w in range(4):
                    part = air[step + 1, par, cc, :, 128 * w : 128 * w + 128].astype(F32)
                    tok_sky[w, pl.ds(par * 4 * na + cc, na, stride=4), :] = part
                return c

            lax.fori_loop(0, 4, unsort, 0)
            rows = pl.ds(pl.multiple_of(par * 4 * na, 4 * na), 4 * na)
            for w in range(4):
                raw_sky[par, 0, :, 128 * w : 128 * w + 128] = tok_sky[w, rows, :].astype(BF16)
            pltpu.make_async_copy(raw_sky.at[par], sky_out.at[par], out_sem.at[par]).start()

    def sea_part(step, par):
        for copy in put_sea(step, par):
            copy.wait_recv()
        exchange_wait(flux_rx, flux_send, flux_recv, step, par, 1, True)
        got = flux_rx[step, par].reshape(2 * no, 128)
        fields = jnp.where(lane < 64, got[:no], got[no:])

        def line(row, c):
            cells = pl.ds(pl.multiple_of(row * 8, 8), 8)
            lhs = (cellw[cells] * fields[None]).astype(BF16).reshape(8 * no, 128)
            z = jnp.dot(lhs, into_wide[...], preferred_element_type=F32).reshape(8, no, 256)
            for i in range(3):
                for j in range(3):
                    tap = v_sea_filter[3 * i + j : 3 * i + j + 1, :]
                    z = z + tap[None] * ocean[step, par, row + i, j : j + 8].astype(F32)
            u = normed(z.reshape(8 * no, 256), v_sea_gain[...])
            hidden = gelu(jnp.dot(u, v_sea_in[...], preferred_element_type=F32)).astype(BF16)
            change = jnp.dot(hidden, v_sea_back[...], preferred_element_type=F32).reshape(8, no, 256)
            old = ocean[step, par, row + 1, 1:9].astype(F32)
            ocean[step + 1, par, row + 1, 1:9] = (old + seaw[cells] * change).astype(BF16)
            return c

        lax.fori_loop(0, 4, line, 0)

        @pl.when(step + 1 < NSTEP)
        def _():
            make_sst(step + 1, par)
            send_sst(step + 1, par)

        @pl.when(step + 1 == NSTEP)
        def _():
            pltpu.make_async_copy(
                ocean.at[step + 1, par, pl.ds(1, 4), pl.ds(1, 8)], sea_out.at[par], out_sem.at[2 + par]
            ).start()

    def one_step(step, c):
        def sky_loop(par, c):
            sky_part(step, par)
            return c

        def sea_loop(par, c):
            sea_part(step, par)
            return c

        lax.fori_loop(0, 2, sky_loop, 0)

        @pl.when(step + 1 < NSTEP)
        def _():
            for par in range(2):
                start(put_air(step + 1, par))

        start(put_sea(step, 1))
        lax.fori_loop(0, 2, sea_loop, 0)

        @pl.when(step + 1 < NSTEP)
        def _():
            start(put_sea(step + 1, 0))

        return c

    lax.fori_loop(0, NSTEP, one_step, 0)

    def close(n, c):
        step, par = n // 2, lax.rem(n, 2)
        for copy in put_air(step, par) + put_sea(step, par):
            copy.wait_send()
        exchange_wait(sst_tx, sst_send, sst_recv, step, par, 0, False)
        exchange_wait(flux_tx, flux_send, flux_recv, step, par, 1, False)
        return c

    lax.fori_loop(0, 2 * NSTEP, close, 0)
    for par in range(2):
        pltpu.make_async_copy(raw_sky.at[par], sky_out.at[par], out_sem.at[par]).wait()
        pltpu.make_async_copy(
            ocean.at[NSTEP, par, pl.ds(1, 4), pl.ds(1, 8)], sea_out.at[par], out_sem.at[2 + par]
        ).wait()


def local(na, no, sky, sea, above, beneath, cover, sea_flag, sky_filter, sky_gain, heat, sky_in, sky_back, to_flux,
          sea_filter, sea_gain, from_flux, sea_in, sea_back, to_sst):
    smem = pl.BlockSpec(memory_space=pltpu.SMEM)
    hbm = pl.BlockSpec(memory_space=pl.ANY)
    vmem = pltpu.VMEM
    dma = pltpu.SemaphoreType.DMA
    n, p = NSTEP, 2
    big = [sky, sea, sky_filter, sky_gain[None], heat, sky_in, sky_back, to_flux.T, sea_filter, sea_gain[None], from_flux, sea_in,
           sea_back, to_sst.T]
    sky_new, sea_new = pl.pallas_call(
        functools.partial(kernel, na, no),
        out_shape=(
            jax.ShapeDtypeStruct(sky.shape, BF16),
            jax.ShapeDtypeStruct((p, 4, 8, no, 256), BF16),
        ),
        in_specs=[smem] * 4 + [hbm] * len(big),
        out_specs=(hbm, hbm),
        scratch_shapes=[vmem(x.shape, x.dtype) for x in big] + [
            vmem((4, p * 4 * na, 128), F32),
            vmem((2, 2 * no * 32, 128), F32),
            vmem((n + 1, p, 4, na, 512), BF16),
            vmem((n, p, 4, na, 512), BF16),
            vmem((n, p, 4, na, 512), BF16),
            vmem((n + 1, p, 6, 10, no, 256), BF16),
            vmem((3, 6, na, 512), F32),
            vmem((4, na, 512), F32),
            vmem((4, na, 512), BF16),
            vmem((4 * na, 1024), BF16),
            vmem((512, 128), BF16),
            vmem((128, 512), BF16),
            vmem((128, 256), BF16),
            vmem((256, 128), BF16),
            vmem((32, no, 128), F32),
            vmem((32, no, 256), F32),
            vmem((32, no, 256), F32),
            vmem((n, p, na, 1, 128), F32),
            vmem((n, p, na, 1, 128), F32),
            vmem((n, p, na, 1, 128), F32),
            vmem((n, p, na, 1, 128), F32),
            dma((len(big),)),
            dma((n, p)),
            dma((n, p)),
            dma((n, p)),
            dma((n, p)),
            dma((n, p, 2)),
            dma((n, p, 2)),
            dma((n, p, 2)),
            dma((n, p, 8)),
            dma((n, p, 8)),
            dma((4,)),
        ],
        compiler_params=pltpu.CompilerParams(
            collective_id=0, has_side_effects=True, vmem_limit_bytes=56 * 1024 * 1024
        ),
        name="coupled_steps",
    )(above, beneath, cover.transpose(0, 2, 1), sea_flag, *big)
    sea_new = sea_new.transpose(3, 0, 1, 2, 4).reshape(sea.shape)
    return sky_new, sea_new


def solution(mesh):
    return jax.shard_map(
        functools.partial(local, mesh.shape["atm"], mesh.shape["ocn"]),
        mesh=mesh,
        in_specs=(
            P("ocn", "atm", None, None),
            P(None, "ocn", "atm", None),
            P("atm"),
            P("atm"),
            P("ocn", "atm", None),
            P("ocn", "atm"),
        ) + (P(),) * 12,
        out_specs=(P("ocn", "atm", None, None), P(None, "ocn", "atm", None)),
        check_vma=False,
    )
```

```python
import functools

import jax
import jax.numpy as jnp
from jax import lax
from jax.experimental import pallas as pl
from jax.experimental.pallas import tpu as pltpu
from jax.sharding import PartitionSpec as P

MESH = pl.DeviceIdType.MESH
F32 = jnp.float32
BF16 = jnp.bfloat16
NSTEP = 2
SIDES = [(-1, 0), (1, 0), (0, -1), (0, 1)]


def gelu_twice(x):
    inner = x * (0.7978845608028654 + 0.035677408136300125 * (x * x))
    return x * (1.0 + jnp.tanh(inner))


def normed(z, gain):
    shifted = z - jnp.mean(z, axis=-1, keepdims=True)
    spread = jnp.mean(shifted * shifted, axis=-1, keepdims=True)
    return (shifted * lax.rsqrt(spread + 1e-05) * gain).astype(BF16)


def spread_over_lanes(rows, lanes):
    r = lax.broadcasted_iota(jnp.int32, (rows, lanes), 0)
    c = lax.broadcasted_iota(jnp.int32, (rows, lanes), 1)
    return (lax.rem(c, rows) == r).astype(BF16)


def kernel(
    na, no,
    above, beneath, cover, sea_flag,
    sky, sea, sky_filter, sky_gain, heat, sky_in, sky_back, to_flux, sea_filter, sea_gain, from_flux, sea_in, sea_back, to_sst,
    sky_out, sea_out,
    raw_sky, raw_sea, v_sky_filter, v_sky_gain, v_heat, v_sky_in, v_sky_back, v_to_flux, v_sea_filter, v_sea_gain, v_from_flux,
    v_sea_in, v_sea_back, v_to_sst,
    tok_sky, tok_sea, air, up, down, ocean, share_tx, share_rx, ext, zbuf, ubuf, hbuf, zsea, usea, hsea,
    flux_wide, heat_wide, into_wide, sst_wide, cellw, seaw, poolw,
    sst_tx, sst_rx, flux_tx, flux_rx,
    in_sem, sst_send, sst_recv, flux_send, flux_recv, self_sem, air_send, air_recv, sea_send, sea_recv, out_sem,
):
    a = lax.axis_index("atm")
    o = lax.axis_index("ocn")
    half_a = a // 2
    mine = half_a == o

    def at(atm, ocn):
        return {"atm": lax.rem(atm + na, na), "ocn": lax.rem(ocn + no, no)}

    def is_me(atm, ocn):
        return jnp.logical_and(atm == a, ocn == o)

    loads = [
        pltpu.make_async_copy(src, dst, in_sem.at[n])
        for n, (src, dst) in enumerate([
            (sea, raw_sea), (sky, raw_sky), (to_sst, v_to_sst), (sky_filter, v_sky_filter), (heat, v_heat),
            (sky_gain, v_sky_gain), (sky_in, v_sky_in), (sky_back, v_sky_back), (to_flux, v_to_flux),
            (sea_filter, v_sea_filter), (sea_gain, v_sea_gain), (from_flux, v_from_flux), (sea_in, v_sea_in),
            (sea_back, v_sea_back),
        ])
    ]
    for load in loads:
        load.start()

    barrier = pltpu.get_barrier_semaphore()

    def greet(n, c):
        pl.semaphore_signal(barrier, inc=1, device_id=at(a + n, half_a), device_id_type=MESH)
        return c

    lax.fori_loop(1, na, greet, 0)

    @pl.when(jnp.logical_not(mine))
    def _():
        pl.semaphore_signal(barrier, inc=1, device_id=at(a, half_a), device_id_type=MESH)

    for di, dj in SIDES:
        pl.semaphore_signal(barrier, inc=1, device_id=at(a + dj, o + di), device_id_type=MESH)

    lane = lax.broadcasted_iota(jnp.int32, (no, 128), 1)

    def pool_table(cell, c):
        row, col = cell // 8, lax.rem(cell, 8)
        flag = jnp.full((no, 256), sea_flag[row, col], jnp.int32).astype(F32)
        r0, c0 = row // 2 * 2, col // 2 * 2
        count = sea_flag[r0, c0] + sea_flag[r0, c0 + 1] + sea_flag[r0 + 1, c0] + sea_flag[r0 + 1, c0 + 1]
        count = jnp.full((no, 256), count, jnp.int32).astype(F32)
        seaw[cell] = 0.5 * flag
        poolw[cell] = flag / jnp.maximum(count, 1.0)
        return c

    lax.fori_loop(0, 32, pool_table, 0)

    def cell_table(cell, c):
        row, col = cell // 8, lax.rem(cell, 8)
        share = jnp.zeros((no, 128), F32)
        for k in range(4):
            share = share + jnp.where(lane // 16 == cover[row, k, col], 0.25, 0.0)
        cellw[cell] = share
        return c

    loads[0].wait()
    per = 2 * no // 4

    def open_sea(n, c):
        part = raw_sea[pl.ds(n * per, per)].astype(F32)
        part = part.reshape(per * 32, 256)
        for w in range(2):
            tok_sea[w, pl.ds(pl.multiple_of(n * per * 32, per * 32), per * 32), :] = part[:, 128 * w : 128 * w + 128]
        return c

    lax.fori_loop(0, 4, open_sea, 0)

    def sort_sea(par):
        def sort_cell(cell, c):
            row, col = cell // 8, lax.rem(cell, 8)
            for w in range(2):
                part = tok_sea[w, pl.ds(par * 32 + cell, no, stride=64), :]
                ocean[0, par, 1 + row, 1 + col, :, 128 * w : 128 * w + 128] = part.astype(BF16)
            return c

        lax.fori_loop(0, 32, sort_cell, 0)

    loads[2].wait()
    sst_wide[...] = lax.dot_general(
        v_to_sst[...], spread_over_lanes(8, 128), (((0,), (0,)), ((), ())), preferred_element_type=F32
    ).astype(BF16)

    def put_air(step, par):
        return [
            pltpu.make_async_remote_copy(
                src_ref=air.at[step, par], dst_ref=there.at[step, par], send_sem=air_send.at[step, par, n],
                recv_sem=air_recv.at[step, par, n], device_id=at(a + da, o), device_id_type=MESH,
            )
            for n, (there, da) in enumerate([(up, 1), (down, -1)])
        ]

    def put_cols(step, par):
        return [
            pltpu.make_async_remote_copy(
                src_ref=ocean.at[step, par, pl.ds(1, 4), src], dst_ref=ocean.at[step, par, pl.ds(1, 4), dst],
                send_sem=sea_send.at[step, par, n], recv_sem=sea_recv.at[step, par, n],
                device_id=at(a + da, o), device_id_type=MESH,
            )
            for n, (src, dst, da) in enumerate([(8, 0, 1), (1, 9, -1)])
        ]

    def put_rows(step, par):
        return [
            pltpu.make_async_remote_copy(
                src_ref=share_tx.at[step, par, n], dst_ref=share_rx.at[step, par, n],
                send_sem=sea_send.at[step, par, 2 + n], recv_sem=sea_recv.at[step, par, 2 + n],
                device_id=at(a, o + do), device_id_type=MESH,
            )
            for n, do in enumerate([1, -1])
        ]

    def send_rows(step, par):
        for copy in put_cols(step, par):
            copy.wait_recv()
        for n, (row, i) in enumerate([(4, 0), (1, 2)]):
            for w in range(2):
                part = slice(128 * w, 128 * w + 128)
                cells = ocean[step, par, row, :, :, part].astype(F32)
                z = jnp.zeros((8, no, 128), F32)
                for j in range(3):
                    z = z + v_sea_filter[3 * i + j : 3 * i + j + 1, part][None] * cells[j : j + 8]
                share_tx[step, par, n, :, :, part] = z.astype(BF16)
        start(put_rows(step, par))

    def start(copies):
        for copy in copies:
            copy.start()

    def make_sst(step, par):
        def block_rows(rr, c):
            parts = []
            for cc in range(4):
                sums = jnp.zeros((no, 256), F32)
                for i in range(2):
                    for j in range(2):
                        cell = (2 * rr + i) * 8 + 2 * cc + j
                        sums = sums + poolw[cell] * ocean[step, par, 1 + 2 * rr + i, 1 + 2 * cc + j].astype(F32)
                parts.append(sums.astype(BF16))
            lines = jnp.zeros((no, 128), F32)
            which = lax.rem(lane // 8, 4)
            for cc in range(4):
                got = jnp.dot(parts[cc], sst_wide[...], preferred_element_type=F32)
                lines = jnp.where(which == cc, got, lines)
            sst_tx[step, par, pl.ds(rr * no, no)] = lines.reshape(no, 1, 128)
            return c

        for rr in range(2):
            block_rows(rr, 0)

    def send_sst(step, par):
        def put(ocn, rr):
            return pltpu.make_async_remote_copy(
                src_ref=sst_tx.at[step, par, rr * no + ocn], dst_ref=sst_rx.at[step, par, a],
                send_sem=sst_send.at[step, par], recv_sem=sst_recv.at[step, par],
                device_id=at(2 * o + rr, ocn), device_id_type=MESH,
            )

        apart = min(4, no)
        for d in sorted(range(apart), key=lambda d: -min(d, apart - d)):
            def put_group(y, c, d=d):
                ocn = y * apart + lax.rem(o + d, apart)
                if d:
                    for rr in range(2):
                        put(ocn, rr).start()
                else:
                    for rr in range(2):
                        @pl.when(jnp.logical_not(is_me(2 * o + rr, ocn)))
                        def _():
                            put(ocn, rr).start()
                return c

            lax.fori_loop(0, no // apart, put_group, 0)

        @pl.when(mine)
        def _():
            pltpu.make_async_copy(
                sst_tx.at[step, par, lax.rem(a, 2) * no + o], sst_rx.at[step, par, a], self_sem.at[step, par, 0]
            ).start()

    def send_flux(step, par):
        place = lax.rem(a, 2) * no + o

        def put(atm):
            atm = lax.rem(atm + na, na)
            return pltpu.make_async_remote_copy(
                src_ref=flux_tx.at[step, par, atm], dst_ref=flux_rx.at[step, par, place],
                send_sem=flux_send.at[step, par], recv_sem=flux_recv.at[step, par],
                device_id=at(atm, half_a), device_id_type=MESH,
            )

        put(a + na // 2).start()

        def put_pair(n, c):
            put(a + na // 2 + n).start()
            put(a + na // 2 - n).start()
            return c

        lax.fori_loop(1, na // 2, put_pair, 0)

        @pl.when(jnp.logical_not(mine))
        def _():
            put(a).start()

        @pl.when(mine)
        def _():
            pltpu.make_async_copy(
                flux_tx.at[step, par, a], flux_rx.at[step, par, place], self_sem.at[step, par, 1]
            ).start()

    def rows_of(buf, sem_send, sem_recv, step, par, count):
        part = buf.at[step, par, pl.ds(0, count)]
        return pltpu.make_async_remote_copy(
            src_ref=part, dst_ref=part, send_sem=sem_send.at[step, par], recv_sem=sem_recv.at[step, par],
            device_id=at(a, o), device_id_type=MESH,
        )

    def exchange_wait(buf, sem_send, sem_recv, step, par, n, received):
        @pl.when(mine)
        def _():
            copy = rows_of(buf, sem_send, sem_recv, step, par, na - 1)
            if received:
                pltpu.make_async_copy(buf.at[step, par, 0], buf.at[step, par, 0], self_sem.at[step, par, n]).wait()
                copy.wait_recv()
            else:
                copy.wait_send()

        @pl.when(jnp.logical_not(mine))
        def _():
            copy = rows_of(buf, sem_send, sem_recv, step, par, na)
            if received:
                copy.wait_recv()
            else:
                copy.wait_send()


    sort_sea(0)
    make_sst(0, 0)

    @pl.when(mine)
    def _():
        pl.semaphore_wait(barrier, na + 3)

    @pl.when(jnp.logical_not(mine))
    def _():
        pl.semaphore_wait(barrier, na + 4)

    send_sst(0, 0)
    sort_sea(1)
    make_sst(0, 1)
    send_sst(0, 1)
    loads[1].wait()
    for w in range(4):
        tok_sky[w] = raw_sky[:, :, :, 128 * w : 128 * w + 128].astype(F32).reshape(8 * na, 128)

    def sort_sky(cc, c):
        for par in range(2):
            for w in range(4):
                part = tok_sky[w, pl.ds(par * 4 * na + cc, na, stride=4), :]
                air[0, par, cc, :, 128 * w : 128 * w + 128] = part.astype(BF16)
        return c

    lax.fori_loop(0, 4, sort_sky, 0)

    for par in range(2):
        start(put_cols(0, par))
        start(put_air(0, par))

    lax.fori_loop(0, 32, cell_table, 0)

    for load in loads[3:]:
        load.wait()
    flux_wide[...] = lax.dot_general(
        v_to_flux[...], spread_over_lanes(16, 128), (((0,), (0,)), ((), ())), preferred_element_type=F32
    ).astype(BF16)
    heat_wide[...] = lax.dot_general(
        spread_over_lanes(8, 128), v_heat[...].astype(BF16), (((0,), (0,)), ((), ())), preferred_element_type=F32
    ).astype(BF16)
    into_wide[...] = lax.dot_general(
        spread_over_lanes(16, 128), v_from_flux[...].astype(BF16), (((0,), (0,)), ((), ())), preferred_element_type=F32
    ).astype(BF16)

    send_rows(0, 0)

    turns = []
    for code in (above[0], beneath[0]):
        cosine = jnp.where(code == 0, 1.0, 0.0) - jnp.where(code == 2, 1.0, 0.0)
        sine = jnp.where(code == 1, 1.0, 0.0) - jnp.where(code == 3, 1.0, 0.0)
        turns.append((cosine, sine))

    lane_a = lax.broadcasted_iota(jnp.int32, (na, 128), 1)

    def sky_part(step, par):
        for copy in put_air(step, par):
            copy.wait_recv()

        def frame(cc, c):
            ext[1, cc + 1] = air[step, par, cc].astype(F32)
            for n, src in ((0, up), (2, down)):
                cosine, sine = turns[n // 2]
                east = src[step, par, cc, :, :256].astype(F32)
                north = src[step, par, cc, :, 256:].astype(F32)
                ext[n, cc + 1, :, :256] = cosine * east - sine * north
                ext[n, cc + 1, :, 256:] = sine * east + cosine * north
            return c

        lax.fori_loop(0, 4, frame, 0)

        def ends(n, c):
            ext[n, 0] = pltpu.roll(ext[n, 4], 1, 0)
            ext[n, 5] = pltpu.roll(ext[n, 1], na - 1, 0)
            return c

        lax.fori_loop(0, 3, ends, 0)

        exchange_wait(sst_rx, sst_send, sst_recv, step, par, 0, True)
        fields = sst_rx[step, par].reshape(na, 128)
        for cc in range(4):
            one = jnp.where(lane_a // 8 == cc, fields, 0.0).astype(BF16)
            zbuf[cc] = jnp.dot(one, heat_wide[...], preferred_element_type=F32)

        def column(cc, c):
            for w in range(2):
                part = slice(256 * w, 256 * w + 256)
                z = zbuf[cc, :, part]
                for i in range(3):
                    for j in range(3):
                        z = z + v_sky_filter[3 * i + j : 3 * i + j + 1, part] * ext[i, cc + j, :, part]
                zbuf[cc, :, part] = z
            return c

        lax.fori_loop(0, 4, column, 0)
        ubuf[...] = normed(zbuf[...].reshape(4 * na, 512), v_sky_gain[...])
        for n in range(4):
            part = slice(256 * n, 256 * n + 256)
            hbuf[:, part] = gelu_twice(jnp.dot(ubuf[...], v_sky_in[:, part], preferred_element_type=F32)).astype(BF16)
        for n in range(2):
            part = slice(256 * n, 256 * n + 256)
            change = 0.5 * jnp.dot(hbuf[...], v_sky_back[:, part], preferred_element_type=F32)
            old = air[step, par, :, :, part].astype(F32)
            air[step + 1, par, :, :, part] = (old + change.reshape(4, na, 256)).astype(BF16)
        lines = jnp.zeros((na, 128), F32)
        for cc in range(4):
            got = jnp.dot(air[step + 1, par, cc], flux_wide[...], preferred_element_type=F32)
            lines = jnp.where(lax.rem(lane_a // 16, 4) == cc, got, lines)
        flux_tx[step, par] = lines.reshape(na, 1, 128)
        send_flux(step, par)

        @pl.when(step + 1 == NSTEP)
        def _():
            def unsort(cc, c):
                for w in range(4):
                    part = air[step + 1, par, cc, :, 128 * w : 128 * w + 128].astype(F32)
                    tok_sky[w, pl.ds(par * 4 * na + cc, na, stride=4), :] = part
                return c

            lax.fori_loop(0, 4, unsort, 0)
            rows = pl.ds(pl.multiple_of(par * 4 * na, 4 * na), 4 * na)
            for w in range(4):
                raw_sky[par, 0, :, 128 * w : 128 * w + 128] = tok_sky[w, rows, :].astype(BF16)
            pltpu.make_async_copy(raw_sky.at[par], sky_out.at[par], out_sem.at[par]).start()

    def sea_part(step, par):
        exchange_wait(flux_rx, flux_send, flux_recv, step, par, 1, True)
        got = flux_rx[step, par].reshape(2 * no, 128)
        fields = jnp.where(lane < 64, got[:no], got[no:])

        lhs = (cellw[...] * fields[None]).astype(BF16).reshape(32 * no, 128)
        zsea[...] = jnp.dot(lhs, into_wide[...], preferred_element_type=F32).reshape(4, 8 * no, 256)

        def line(row, c, taps=(0, 1, 2), side=None):
            for w in range(2):
                part = slice(128 * w, 128 * w + 128)
                z = zsea[row, :, part].reshape(8, no, 128)
                if side is not None:
                    z = z + share_rx[step, par, side, :, :, part].astype(F32)
                for i in taps:
                    cells = ocean[step, par, row + i, :, :, part].astype(F32)
                    for j in range(3):
                        z = z + v_sea_filter[3 * i + j : 3 * i + j + 1, part][None] * cells[j : j + 8]
                zsea[row, :, part] = z.reshape(8 * no, 128)
            return c

        lax.fori_loop(1, 3, line, 0)
        for copy in put_rows(step, par):
            copy.wait_recv()
        line(0, 0, (1, 2), 0)
        line(3, 0, (0, 1), 1)
        rows = 16 * no
        for m in range(2):
            usea[rows * m : rows * m + rows] = normed(zsea[2 * m : 2 * m + 2].reshape(rows, 256), v_sea_gain[...])
        for m in range(2):
            for n in range(2):
                part = slice(256 * n, 256 * n + 256)
                got = jnp.dot(usea[rows * m : rows * m + rows], v_sea_in[:, part], preferred_element_type=F32)
                hsea[rows * m : rows * m + rows, part] = gelu_twice(got).astype(BF16)
        for m in range(2):
            change = jnp.dot(hsea[rows * m : rows * m + rows], v_sea_back[...], preferred_element_type=F32)
            change = change.reshape(2, 8, no, 256) * seaw[16 * m : 16 * m + 16].reshape(2, 8, no, 256)
            old = ocean[step, par, 1 + 2 * m : 3 + 2 * m, 1:9].astype(F32)
            ocean[step + 1, par, 1 + 2 * m : 3 + 2 * m, 1:9] = (old + change).astype(BF16)

        @pl.when(step + 1 < NSTEP)
        def _():
            make_sst(step + 1, par)
            send_sst(step + 1, par)
            start(put_cols(step + 1, par))

        @pl.when(step + 1 == NSTEP)
        def _():
            pltpu.make_async_copy(
                ocean.at[step + 1, par, pl.ds(1, 4), pl.ds(1, 8)], sea_out.at[par], out_sem.at[2 + par]
            ).start()

    def one_step(step, c):
        def sky_loop(par, c):
            sky_part(step, par)
            return c

        def sea_loop(par, c):
            sea_part(step, par)
            return c

        lax.fori_loop(0, 2, sky_loop, 0)

        @pl.when(step + 1 < NSTEP)
        def _():
            for par in range(2):
                start(put_air(step + 1, par))

        send_rows(step, 1)
        lax.fori_loop(0, 2, sea_loop, 0)

        @pl.when(step + 1 < NSTEP)
        def _():
            send_rows(step + 1, 0)

        return c

    lax.fori_loop(0, NSTEP, one_step, 0)

    def close(n, c):
        step, par = n // 2, lax.rem(n, 2)
        for copy in put_air(step, par) + put_cols(step, par) + put_rows(step, par):
            copy.wait_send()
        exchange_wait(sst_tx, sst_send, sst_recv, step, par, 0, False)
        exchange_wait(flux_tx, flux_send, flux_recv, step, par, 1, False)
        return c

    lax.fori_loop(0, 2 * NSTEP, close, 0)
    for par in range(2):
        pltpu.make_async_copy(raw_sky.at[par], sky_out.at[par], out_sem.at[par]).wait()
        pltpu.make_async_copy(
            ocean.at[NSTEP, par, pl.ds(1, 4), pl.ds(1, 8)], sea_out.at[par], out_sem.at[2 + par]
        ).wait()


def local(na, no, sky, sea, above, beneath, cover, sea_flag, sky_filter, sky_gain, heat, sky_in, sky_back, to_flux,
          sea_filter, sea_gain, from_flux, sea_in, sea_back, to_sst):
    smem = pl.BlockSpec(memory_space=pltpu.SMEM)
    hbm = pl.BlockSpec(memory_space=pl.ANY)
    vmem = pltpu.VMEM
    dma = pltpu.SemaphoreType.DMA
    n, p = NSTEP, 2
    big = [sky, sea, sky_filter, sky_gain[None], heat, sky_in, sky_back, to_flux.T, sea_filter, sea_gain[None], from_flux, sea_in,
           sea_back, to_sst.T]
    sky_new, sea_new = pl.pallas_call(
        functools.partial(kernel, na, no),
        out_shape=(
            jax.ShapeDtypeStruct(sky.shape, BF16),
            jax.ShapeDtypeStruct((p, 4, 8, no, 256), BF16),
        ),
        in_specs=[smem] * 4 + [hbm] * len(big),
        out_specs=(hbm, hbm),
        scratch_shapes=[vmem(x.shape, x.dtype) for x in big] + [
            vmem((4, p * 4 * na, 128), F32),
            vmem((2, 2 * no * 32, 128), F32),
            vmem((n + 1, p, 4, na, 512), BF16),
            vmem((n, p, 4, na, 512), BF16),
            vmem((n, p, 4, na, 512), BF16),
            vmem((n + 1, p, 6, 10, no, 256), BF16),
            vmem((n, p, 2, 8, no, 256), BF16),
            vmem((n, p, 2, 8, no, 256), BF16),
            vmem((3, 6, na, 512), F32),
            vmem((4, na, 512), F32),
            vmem((4 * na, 512), BF16),
            vmem((4 * na, 1024), BF16),
            vmem((4, 8 * no, 256), F32),
            vmem((32 * no, 256), BF16),
            vmem((32 * no, 512), BF16),
            vmem((512, 128), BF16),
            vmem((128, 512), BF16),
            vmem((128, 256), BF16),
            vmem((256, 128), BF16),
            vmem((32, no, 128), F32),
            vmem((32, no, 256), F32),
            vmem((32, no, 256), F32),
            vmem((n, p, na, 1, 128), F32),
            vmem((n, p, na, 1, 128), F32),
            vmem((n, p, na, 1, 128), F32),
            vmem((n, p, na, 1, 128), F32),
            dma((len(big),)),
            dma((n, p)),
            dma((n, p)),
            dma((n, p)),
            dma((n, p)),
            dma((n, p, 2)),
            dma((n, p, 2)),
            dma((n, p, 2)),
            dma((n, p, 4)),
            dma((n, p, 4)),
            dma((4,)),
        ],
        compiler_params=pltpu.CompilerParams(
            collective_id=0, has_side_effects=True, vmem_limit_bytes=56 * 1024 * 1024
        ),
        name="coupled_steps",
    )(above, beneath, cover.transpose(0, 2, 1), sea_flag, *big)
    sea_new = sea_new.transpose(3, 0, 1, 2, 4).reshape(sea.shape)
    return sky_new, sea_new


def solution(mesh):
    return jax.shard_map(
        functools.partial(local, mesh.shape["atm"], mesh.shape["ocn"]),
        mesh=mesh,
        in_specs=(
            P("ocn", "atm", None, None),
            P(None, "ocn", "atm", None),
            P("atm"),
            P("atm"),
            P("ocn", "atm", None),
            P("ocn", "atm"),
        ) + (P(),) * 12,
        out_specs=(P("ocn", "atm", None, None), P(None, "ocn", "atm", None)),
        check_vma=False,
    )
```

```python
import functools

import jax
import jax.numpy as jnp
from jax import lax
from jax.experimental import pallas as pl
from jax.experimental.pallas import tpu as pltpu
from jax.sharding import PartitionSpec as P

MESH = pl.DeviceIdType.MESH
F32 = jnp.float32
BF16 = jnp.bfloat16
NSTEP = 2
SIDES = [(-1, 0), (1, 0), (0, -1), (0, 1)]


def gelu_twice(x):
    inner = x * (0.7978845608028654 + 0.035677408136300125 * (x * x))
    return x * (1.0 + jnp.tanh(inner))


def normed(z, gain):
    shifted = z - jnp.mean(z, axis=-1, keepdims=True)
    spread = jnp.mean(shifted * shifted, axis=-1, keepdims=True)
    return (shifted * lax.rsqrt(spread + 1e-05) * gain).astype(BF16)


def spread_over_lanes(rows, lanes):
    r = lax.broadcasted_iota(jnp.int32, (rows, lanes), 0)
    c = lax.broadcasted_iota(jnp.int32, (rows, lanes), 1)
    return (lax.rem(c, rows) == r).astype(BF16)


def kernel(
    na, no,
    above_in, beneath_in, cover_in, flag_in,
    sky, sea, sky_filter, sky_gain, heat, sky_in, sky_back, to_flux, sea_filter, sea_gain, from_flux, sea_in, sea_back, to_sst,
    sky_out, sea_out,
    above, beneath, cover, sea_flag,
    raw_sky, raw_sea, v_sky_filter, v_sky_gain, v_heat, v_sky_in, v_sky_back, v_to_flux, v_sea_filter, v_sea_gain, v_from_flux,
    v_sea_in, v_sea_back, v_to_sst,
    tok_sky, tok_sea, air, up, down, ocean, share_tx, share_rx, ext, zbuf, ubuf, hbuf, zsea, usea, hsea,
    flux_wide, heat_wide, into_wide, sst_wide, cellw, seaw, poolw,
    sst_tx, sst_rx, flux_tx, flux_rx,
    in_sem, sst_send, sst_recv, flux_send, flux_recv, self_sem, air_send, air_recv, sea_send, sea_recv, out_sem,
):
    a = lax.axis_index("atm")
    o = lax.axis_index("ocn")
    half_a = a // 2
    mine = half_a == o

    def at(atm, ocn):
        return {"atm": lax.rem(atm + na, na), "ocn": lax.rem(ocn + no, no)}

    def is_me(atm, ocn):
        return jnp.logical_and(atm == a, ocn == o)

    loads = [
        pltpu.make_async_copy(src, dst, in_sem.at[n])
        for n, (src, dst) in enumerate([
            (sea.at[:, 0], raw_sea.at[0]), (sky, raw_sky), (to_sst, v_to_sst), (sky_filter, v_sky_filter), (heat, v_heat),
            (sky_gain, v_sky_gain), (sky_in, v_sky_in), (sky_back, v_sky_back), (to_flux, v_to_flux),
            (sea_filter, v_sea_filter), (sea_gain, v_sea_gain), (from_flux, v_from_flux), (sea_in, v_sea_in),
            (sea_back, v_sea_back), (flag_in, sea_flag), (cover_in, cover), (above_in, above), (beneath_in, beneath),
            (sea.at[:, 1], raw_sea.at[1]),
        ])
    ]
    loads[0].start()
    loads[14].start()
    loads[18].start()

    barrier = pltpu.get_barrier_semaphore()

    def greet(n, c):
        pl.semaphore_signal(barrier, inc=1, device_id=at(a + n, half_a), device_id_type=MESH)
        return c

    lax.fori_loop(1, na, greet, 0)

    @pl.when(jnp.logical_not(mine))
    def _():
        pl.semaphore_signal(barrier, inc=1, device_id=at(a, half_a), device_id_type=MESH)

    for di, dj in SIDES:
        pl.semaphore_signal(barrier, inc=1, device_id=at(a + dj, o + di), device_id_type=MESH)

    for load in loads[1:14] + loads[15:18]:
        load.start()

    lane = lax.broadcasted_iota(jnp.int32, (no, 128), 1)

    def pool_table(cell, c):
        row, col = cell // 8, lax.rem(cell, 8)
        flag = jnp.full((no, 256), sea_flag[row, col], jnp.int32).astype(F32)
        r0, c0 = row // 2 * 2, col // 2 * 2
        count = sea_flag[r0, c0] + sea_flag[r0, c0 + 1] + sea_flag[r0 + 1, c0] + sea_flag[r0 + 1, c0 + 1]
        count = jnp.full((no, 256), count, jnp.int32).astype(F32)
        seaw[cell] = 0.5 * flag
        poolw[cell] = flag / jnp.maximum(count, 1.0)
        return c

    loads[14].wait()
    lax.fori_loop(0, 32, pool_table, 0)

    def cell_table(cell, c):
        row, col = cell // 8, lax.rem(cell, 8)
        share = jnp.zeros((no, 128), F32)
        for k in range(4):
            share = share + jnp.where(lane // 16 == cover[row, k, col], 0.25, 0.0)
        cellw[cell] = share
        return c

    def open_sea(par):
        loads[18 * par].wait()
        for w in range(2):
            part = raw_sea[par, :, :, :, 128 * w : 128 * w + 128].astype(F32)
            tok_sea[par, w] = part.reshape(32 * no, 128)

    def sort_sea(par):
        open_sea(par)

        def sort_cell(cell, c):
            row, col = cell // 8, lax.rem(cell, 8)
            for w in range(2):
                part = tok_sea[par, w, pl.ds(cell, no, stride=32), :]
                ocean[0, par, 1 + row, 1 + col, :, 128 * w : 128 * w + 128] = part.astype(BF16)
            return c

        lax.fori_loop(0, 32, sort_cell, 0)

    loads[2].wait()
    sst_wide[...] = lax.dot_general(
        v_to_sst[...], spread_over_lanes(8, 128), (((0,), (0,)), ((), ())), preferred_element_type=F32
    ).astype(BF16)

    def put_air(step, par):
        return [
            pltpu.make_async_remote_copy(
                src_ref=air.at[step, par], dst_ref=there.at[step, par], send_sem=air_send.at[step, par, n],
                recv_sem=air_recv.at[step, par, n], device_id=at(a + da, o), device_id_type=MESH,
            )
            for n, (there, da) in enumerate([(up, 1), (down, -1)])
        ]

    def put_cols(step, par):
        return [
            pltpu.make_async_remote_copy(
                src_ref=ocean.at[step, par, pl.ds(1, 4), src], dst_ref=ocean.at[step, par, pl.ds(1, 4), dst],
                send_sem=sea_send.at[step, par, n], recv_sem=sea_recv.at[step, par, n],
                device_id=at(a + da, o), device_id_type=MESH,
            )
            for n, (src, dst, da) in enumerate([(8, 0, 1), (1, 9, -1)])
        ]

    def put_rows(step, par):
        return [
            pltpu.make_async_remote_copy(
                src_ref=share_tx.at[step, par, n], dst_ref=share_rx.at[step, par, n],
                send_sem=sea_send.at[step, par, 2 + n], recv_sem=sea_recv.at[step, par, 2 + n],
                device_id=at(a, o + do), device_id_type=MESH,
            )
            for n, do in enumerate([1, -1])
        ]

    def send_rows(step, par):
        for copy in put_cols(step, par):
            copy.wait_recv()
        for n, (row, i) in enumerate([(4, 0), (1, 2)]):
            for w in range(2):
                part = slice(128 * w, 128 * w + 128)
                cells = ocean[step, par, row, :, :, part].astype(F32)
                z = jnp.zeros((8, no, 128), F32)
                for j in range(3):
                    z = z + v_sea_filter[3 * i + j : 3 * i + j + 1, part][None] * cells[j : j + 8]
                share_tx[step, par, n, :, :, part] = z.astype(BF16)
        start(put_rows(step, par))

    def start(copies):
        for copy in copies:
            copy.start()

    def make_sst(step, par):
        def block_rows(rr, c):
            parts = []
            for cc in range(4):
                sums = jnp.zeros((no, 256), F32)
                for i in range(2):
                    for j in range(2):
                        cell = (2 * rr + i) * 8 + 2 * cc + j
                        sums = sums + poolw[cell] * ocean[step, par, 1 + 2 * rr + i, 1 + 2 * cc + j].astype(F32)
                parts.append(sums.astype(BF16))
            lines = jnp.zeros((no, 128), F32)
            which = lax.rem(lane // 8, 4)
            for cc in range(4):
                got = jnp.dot(parts[cc], sst_wide[...], preferred_element_type=F32)
                lines = jnp.where(which == cc, got, lines)
            sst_tx[step, par, pl.ds(rr * no, no)] = lines.reshape(no, 1, 128)
            return c

        for rr in range(2):
            block_rows(rr, 0)

    def send_sst(step, par):
        def put(ocn, rr):
            return pltpu.make_async_remote_copy(
                src_ref=sst_tx.at[step, par, rr * no + ocn], dst_ref=sst_rx.at[step, par, a],
                send_sem=sst_send.at[step, par], recv_sem=sst_recv.at[step, par],
                device_id=at(2 * o + rr, ocn), device_id_type=MESH,
            )

        apart = min(4, no)
        for d in sorted(range(apart), key=lambda d: -min(d, apart - d)):
            def put_group(y, c, d=d):
                ocn = y * apart + lax.rem(o + d, apart)
                if d:
                    for rr in range(2):
                        put(ocn, rr).start()
                else:
                    for rr in range(2):
                        @pl.when(jnp.logical_not(is_me(2 * o + rr, ocn)))
                        def _():
                            put(ocn, rr).start()
                return c

            lax.fori_loop(0, no // apart, put_group, 0)

        @pl.when(mine)
        def _():
            pltpu.make_async_copy(
                sst_tx.at[step, par, lax.rem(a, 2) * no + o], sst_rx.at[step, par, a], self_sem.at[step, par, 0]
            ).start()

    def send_flux(step, par):
        place = lax.rem(a, 2) * no + o

        def put(atm):
            atm = lax.rem(atm + na, na)
            return pltpu.make_async_remote_copy(
                src_ref=flux_tx.at[step, par, atm], dst_ref=flux_rx.at[step, par, place],
                send_sem=flux_send.at[step, par], recv_sem=flux_recv.at[step, par],
                device_id=at(atm, half_a), device_id_type=MESH,
            )

        put(a + na // 2).start()

        def put_pair(n, c):
            put(a + na // 2 + n).start()
            put(a + na // 2 - n).start()
            return c

        lax.fori_loop(1, na // 2, put_pair, 0)

        @pl.when(jnp.logical_not(mine))
        def _():
            put(a).start()

        @pl.when(mine)
        def _():
            pltpu.make_async_copy(
                flux_tx.at[step, par, a], flux_rx.at[step, par, place], self_sem.at[step, par, 1]
            ).start()

    def rows_of(buf, sem_send, sem_recv, step, par, count):
        part = buf.at[step, par, pl.ds(0, count)]
        return pltpu.make_async_remote_copy(
            src_ref=part, dst_ref=part, send_sem=sem_send.at[step, par], recv_sem=sem_recv.at[step, par],
            device_id=at(a, o), device_id_type=MESH,
        )

    def exchange_wait(buf, sem_send, sem_recv, step, par, n, received):
        @pl.when(mine)
        def _():
            copy = rows_of(buf, sem_send, sem_recv, step, par, na - 1)
            if received:
                pltpu.make_async_copy(buf.at[step, par, 0], buf.at[step, par, 0], self_sem.at[step, par, n]).wait()
                copy.wait_recv()
            else:
                copy.wait_send()

        @pl.when(jnp.logical_not(mine))
        def _():
            copy = rows_of(buf, sem_send, sem_recv, step, par, na)
            if received:
                copy.wait_recv()
            else:
                copy.wait_send()


    sort_sea(0)
    make_sst(0, 0)

    @pl.when(mine)
    def _():
        pl.semaphore_wait(barrier, na + 3)

    @pl.when(jnp.logical_not(mine))
    def _():
        pl.semaphore_wait(barrier, na + 4)

    send_sst(0, 0)
    sort_sea(1)
    make_sst(0, 1)
    send_sst(0, 1)
    loads[1].wait()
    for w in range(4):
        tok_sky[w] = raw_sky[:, :, :, 128 * w : 128 * w + 128].astype(F32).reshape(8 * na, 128)

    def sort_sky(cc, c):
        for par in range(2):
            for w in range(4):
                part = tok_sky[w, pl.ds(par * 4 * na + cc, na, stride=4), :]
                air[0, par, cc, :, 128 * w : 128 * w + 128] = part.astype(BF16)
        return c

    lax.fori_loop(0, 4, sort_sky, 0)

    for par in range(2):
        start(put_cols(0, par))
        start(put_air(0, par))

    loads[15].wait()
    lax.fori_loop(0, 32, cell_table, 0)

    for load in loads[3:14] + loads[16:18]:
        load.wait()
    flux_wide[...] = lax.dot_general(
        v_to_flux[...], spread_over_lanes(16, 128), (((0,), (0,)), ((), ())), preferred_element_type=F32
    ).astype(BF16)
    heat_wide[...] = lax.dot_general(
        spread_over_lanes(8, 128), v_heat[...].astype(BF16), (((0,), (0,)), ((), ())), preferred_element_type=F32
    ).astype(BF16)
    into_wide[...] = lax.dot_general(
        spread_over_lanes(16, 128), v_from_flux[...].astype(BF16), (((0,), (0,)), ((), ())), preferred_element_type=F32
    ).astype(BF16)

    send_rows(0, 0)

    turns = []
    for code in (above[0], beneath[0]):
        cosine = jnp.where(code == 0, 1.0, 0.0) - jnp.where(code == 2, 1.0, 0.0)
        sine = jnp.where(code == 1, 1.0, 0.0) - jnp.where(code == 3, 1.0, 0.0)
        turns.append((cosine, sine))

    lane_a = lax.broadcasted_iota(jnp.int32, (na, 128), 1)

    def sky_stencil(step, par):
        for copy in put_air(step, par):
            copy.wait_recv()

        def frame(cc, c):
            ext[1, cc + 1] = air[step, par, cc].astype(F32)
            for n, src in ((0, up), (2, down)):
                cosine, sine = turns[n // 2]
                east = src[step, par, cc, :, :256].astype(F32)
                north = src[step, par, cc, :, 256:].astype(F32)
                ext[n, cc + 1, :, :256] = cosine * east - sine * north
                ext[n, cc + 1, :, 256:] = sine * east + cosine * north
            return c

        lax.fori_loop(0, 4, frame, 0)

        def ends(n, c):
            ext[n, 0] = pltpu.roll(ext[n, 4], 1, 0)
            ext[n, 5] = pltpu.roll(ext[n, 1], na - 1, 0)
            return c

        lax.fori_loop(0, 3, ends, 0)

        def column(cc, c):
            for w in range(2):
                part = slice(256 * w, 256 * w + 256)
                z = jnp.zeros((na, 256), F32)
                for i in range(3):
                    for j in range(3):
                        z = z + v_sky_filter[3 * i + j : 3 * i + j + 1, part] * ext[i, cc + j, :, part]
                zbuf[par, cc, :, part] = z
            return c

        lax.fori_loop(0, 4, column, 0)

    def sky_part(step, par):
        exchange_wait(sst_rx, sst_send, sst_recv, step, par, 0, True)
        fields = sst_rx[step, par].reshape(na, 128)
        lhs = [jnp.where(lane_a // 8 == cc, fields, 0.0).astype(BF16) for cc in range(4)]
        warm = jnp.dot(jnp.concatenate(lhs, axis=0), heat_wide[...], preferred_element_type=F32)
        ubuf[...] = normed(warm + zbuf[par].reshape(4 * na, 512), v_sky_gain[...])
        for n in range(4):
            part = slice(256 * n, 256 * n + 256)
            hbuf[:, part] = gelu_twice(jnp.dot(ubuf[...], v_sky_in[:, part], preferred_element_type=F32)).astype(BF16)
        for n in range(2):
            part = slice(256 * n, 256 * n + 256)
            change = 0.5 * jnp.dot(hbuf[...], v_sky_back[:, part], preferred_element_type=F32)
            old = air[step, par, :, :, part].astype(F32)
            air[step + 1, par, :, :, part] = (old + change.reshape(4, na, 256)).astype(BF16)
        lines = jnp.zeros((na, 128), F32)
        for cc in range(4):
            got = jnp.dot(air[step + 1, par, cc], flux_wide[...], preferred_element_type=F32)
            lines = jnp.where(lax.rem(lane_a // 16, 4) == cc, got, lines)
        flux_tx[step, par] = lines.reshape(na, 1, 128)
        send_flux(step, par)

        @pl.when(step + 1 == NSTEP)
        def _():
            def unsort(cc, c):
                for w in range(4):
                    part = air[step + 1, par, cc, :, 128 * w : 128 * w + 128].astype(F32)
                    tok_sky[w, pl.ds(par * 4 * na + cc, na, stride=4), :] = part
                return c

            lax.fori_loop(0, 4, unsort, 0)
            rows = pl.ds(pl.multiple_of(par * 4 * na, 4 * na), 4 * na)
            for w in range(4):
                raw_sky[par, 0, :, 128 * w : 128 * w + 128] = tok_sky[w, rows, :].astype(BF16)
            pltpu.make_async_copy(raw_sky.at[par], sky_out.at[par], out_sem.at[par]).start()

    def sea_line(step, par, row, taps, side):
        for w in range(2):
            part = slice(128 * w, 128 * w + 128)
            z = jnp.zeros((8, no, 128), F32) if side is None else share_rx[step, par, side, :, :, part].astype(F32)
            for i in taps:
                cells = ocean[step, par, row + i, :, :, part].astype(F32)
                for j in range(3):
                    z = z + v_sea_filter[3 * i + j : 3 * i + j + 1, part][None] * cells[j : j + 8]
            zsea[par, row, :, part] = z.reshape(8 * no, 128)

    def sea_middle(step, par):
        def line(row, c):
            sea_line(step, par, row, (0, 1, 2), None)
            return c

        lax.fori_loop(1, 3, line, 0)

    def sea_edges(step, par):
        for copy in put_rows(step, par):
            copy.wait_recv()
        sea_line(step, par, 0, (1, 2), 0)
        sea_line(step, par, 3, (0, 1), 1)

    def sea_part(step, par):
        exchange_wait(flux_rx, flux_send, flux_recv, step, par, 1, True)
        got = flux_rx[step, par].reshape(2 * no, 128)
        fields = jnp.where(lane < 64, got[:no], got[no:])
        rows = 16 * no
        for m in range(2):
            lhs = (cellw[16 * m : 16 * m + 16] * fields[None]).astype(BF16).reshape(rows, 128)
            forced = jnp.dot(lhs, into_wide[...], preferred_element_type=F32)
            z = forced + zsea[par, 2 * m : 2 * m + 2].reshape(rows, 256)
            usea[rows * m : rows * m + rows] = normed(z, v_sea_gain[...])
        for m in range(2):
            for n in range(2):
                part = slice(256 * n, 256 * n + 256)
                got = jnp.dot(usea[rows * m : rows * m + rows], v_sea_in[:, part], preferred_element_type=F32)
                hsea[rows * m : rows * m + rows, part] = gelu_twice(got).astype(BF16)
        for m in range(2):
            change = jnp.dot(hsea[rows * m : rows * m + rows], v_sea_back[...], preferred_element_type=F32)
            change = change.reshape(2, 8, no, 256) * seaw[16 * m : 16 * m + 16].reshape(2, 8, no, 256)
            old = ocean[step, par, 1 + 2 * m : 3 + 2 * m, 1:9].astype(F32)
            ocean[step + 1, par, 1 + 2 * m : 3 + 2 * m, 1:9] = (old + change).astype(BF16)

        @pl.when(step + 1 < NSTEP)
        def _():
            make_sst(step + 1, par)
            send_sst(step + 1, par)
            start(put_cols(step + 1, par))

        @pl.when(step + 1 == NSTEP)
        def _():
            pltpu.make_async_copy(
                ocean.at[step + 1, par, pl.ds(1, 4), pl.ds(1, 8)], sea_out.at[par], out_sem.at[2 + par]
            ).start()

    def both(step, *parts):
        def run(par, c):
            for part in parts:
                part(step, par)
            return c

        lax.fori_loop(0, 2, run, 0)

    def one_step(step, c):
        both(step, sky_stencil)
        both(step, sky_part)

        @pl.when(step + 1 < NSTEP)
        def _():
            for par in range(2):
                start(put_air(step + 1, par))

        send_rows(step, 1)
        both(step, sea_middle)
        both(step, sea_edges, sea_part)

        @pl.when(step + 1 < NSTEP)
        def _():
            send_rows(step + 1, 0)

        return c

    lax.fori_loop(0, NSTEP, one_step, 0)

    def close(n, c):
        step, par = n // 2, lax.rem(n, 2)
        for copy in put_air(step, par) + put_cols(step, par) + put_rows(step, par):
            copy.wait_send()
        exchange_wait(sst_tx, sst_send, sst_recv, step, par, 0, False)
        exchange_wait(flux_tx, flux_send, flux_recv, step, par, 1, False)
        return c

    lax.fori_loop(0, 2 * NSTEP, close, 0)
    for par in range(2):
        pltpu.make_async_copy(raw_sky.at[par], sky_out.at[par], out_sem.at[par]).wait()
        pltpu.make_async_copy(
            ocean.at[NSTEP, par, pl.ds(1, 4), pl.ds(1, 8)], sea_out.at[par], out_sem.at[2 + par]
        ).wait()


def local(na, no, sky, sea, above, beneath, cover, sea_flag, sky_filter, sky_gain, heat, sky_in, sky_back, to_flux,
          sea_filter, sea_gain, from_flux, sea_in, sea_back, to_sst):
    hbm = pl.BlockSpec(memory_space=pl.ANY)
    vmem = pltpu.VMEM
    dma = pltpu.SemaphoreType.DMA
    n, p = NSTEP, 2
    big = [sky, sea.reshape(no, 2, *sea.shape[1:]), sky_filter, sky_gain[None], heat, sky_in, sky_back, to_flux.T, sea_filter, sea_gain[None], from_flux, sea_in,
           sea_back, to_sst.T]
    small = [above, beneath, cover.transpose(0, 2, 1), sea_flag]
    sky_new, sea_new = pl.pallas_call(
        functools.partial(kernel, na, no),
        out_shape=(
            jax.ShapeDtypeStruct(sky.shape, BF16),
            jax.ShapeDtypeStruct((p, 4, 8, no, 256), BF16),
        ),
        in_specs=[hbm] * (4 + len(big)),
        out_specs=(hbm, hbm),
        scratch_shapes=[pltpu.SMEM(x.shape, x.dtype) for x in small] + [vmem(x.shape, x.dtype) for x in big[:1]] + [
            vmem((2, no, *sea.shape[1:]), BF16)
        ] + [vmem(x.shape, x.dtype) for x in big[2:]] + [
            vmem((4, p * 4 * na, 128), F32),
            vmem((2, 2, no * 32, 128), F32),
            vmem((n + 1, p, 4, na, 512), BF16),
            vmem((n, p, 4, na, 512), BF16),
            vmem((n, p, 4, na, 512), BF16),
            vmem((n + 1, p, 6, 10, no, 256), BF16),
            vmem((n, p, 2, 8, no, 256), BF16),
            vmem((n, p, 2, 8, no, 256), BF16),
            vmem((3, 6, na, 512), F32),
            vmem((p, 4, na, 512), F32),
            vmem((4 * na, 512), BF16),
            vmem((4 * na, 1024), BF16),
            vmem((p, 4, 8 * no, 256), F32),
            vmem((32 * no, 256), BF16),
            vmem((32 * no, 512), BF16),
            vmem((512, 128), BF16),
            vmem((128, 512), BF16),
            vmem((128, 256), BF16),
            vmem((256, 128), BF16),
            vmem((32, no, 128), F32),
            vmem((32, no, 256), F32),
            vmem((32, no, 256), F32),
            vmem((n, p, na, 1, 128), F32),
            vmem((n, p, na, 1, 128), F32),
            vmem((n, p, na, 1, 128), F32),
            vmem((n, p, na, 1, 128), F32),
            dma((len(small) + len(big) + 1,)),
            dma((n, p)),
            dma((n, p)),
            dma((n, p)),
            dma((n, p)),
            dma((n, p, 2)),
            dma((n, p, 2)),
            dma((n, p, 2)),
            dma((n, p, 4)),
            dma((n, p, 4)),
            dma((4,)),
        ],
        compiler_params=pltpu.CompilerParams(
            collective_id=0, has_side_effects=True, vmem_limit_bytes=56 * 1024 * 1024
        ),
        name="coupled_steps",
    )(*small, *big)
    sea_new = sea_new.transpose(3, 0, 1, 2, 4).reshape(sea.shape)
    return sky_new, sea_new


def solution(mesh):
    return jax.shard_map(
        functools.partial(local, mesh.shape["atm"], mesh.shape["ocn"]),
        mesh=mesh,
        in_specs=(
            P("ocn", "atm", None, None),
            P(None, "ocn", "atm", None),
            P("atm"),
            P("atm"),
            P("ocn", "atm", None),
            P("ocn", "atm"),
        ) + (P(),) * 12,
        out_specs=(P("ocn", "atm", None, None), P(None, "ocn", "atm", None)),
        check_vma=False,
    )
```

```python
import functools

import jax
import jax.numpy as jnp
from jax import lax
from jax.experimental import pallas as pl
from jax.experimental.pallas import tpu as pltpu
from jax.sharding import PartitionSpec as P

MESH = pl.DeviceIdType.MESH
F32 = jnp.float32
BF16 = jnp.bfloat16
NSTEP = 2
SIDES = [(-1, 0), (1, 0), (0, -1), (0, 1)]


def gelu_twice(x):
    inner = x * (0.7978845608028654 + 0.035677408136300125 * (x * x))
    return x * (1.0 + jnp.tanh(inner))


def normed(z, gain):
    shifted = z - jnp.mean(z, axis=-1, keepdims=True)
    spread = jnp.mean(shifted * shifted, axis=-1, keepdims=True)
    return (shifted * lax.rsqrt(spread + 1e-05) * gain).astype(BF16)


def spread_over_lanes(rows, lanes):
    r = lax.broadcasted_iota(jnp.int32, (rows, lanes), 0)
    c = lax.broadcasted_iota(jnp.int32, (rows, lanes), 1)
    return (lax.rem(c, rows) == r).astype(BF16)


def kernel(
    na, no,
    above_in, beneath_in, cover_in, flag_in,
    sky, sea, sky_filter, sky_gain, heat, sky_in, sky_back, to_flux, sea_filter, sea_gain, from_flux, sea_in, sea_back, to_sst,
    sky_out, sea_out,
    above, beneath, cover, sea_flag,
    raw_sky, raw_sea, v_sky_filter, v_sky_gain, v_heat, v_sky_in, v_sky_back, v_to_flux, v_sea_filter, v_sea_gain, v_from_flux,
    v_sea_in, v_sea_back, v_to_sst,
    tok_sky, tok_sea, air, up, down, ocean, share_tx, share_rx, ext, zbuf, ubuf, hbuf, zsea, usea, hsea,
    flux_wide, heat_wide, into_wide, sst_wide, cellw, seaw, poolw,
    sst_tx, sst_rx, flux_tx, flux_rx,
    in_sem, sst_send, sst_recv, flux_send, flux_recv, self_sem, air_send, air_recv, sea_send, sea_recv, out_sem,
):
    a = lax.axis_index("atm")
    o = lax.axis_index("ocn")
    half_a = a // 2
    mine = half_a == o

    def at(atm, ocn):
        return {"atm": lax.rem(atm + na, na), "ocn": lax.rem(ocn + no, no)}

    def is_me(atm, ocn):
        return jnp.logical_and(atm == a, ocn == o)

    loads = [
        pltpu.make_async_copy(src, dst, in_sem.at[n])
        for n, (src, dst) in enumerate([
            (sea.at[:, 0], raw_sea.at[0]), (sky, raw_sky), (to_sst, v_to_sst), (sky_filter, v_sky_filter), (heat, v_heat),
            (sky_gain, v_sky_gain), (sky_in, v_sky_in), (sky_back, v_sky_back), (to_flux, v_to_flux),
            (sea_filter, v_sea_filter), (sea_gain, v_sea_gain), (from_flux, v_from_flux), (sea_in, v_sea_in),
            (sea_back, v_sea_back), (flag_in, sea_flag), (cover_in, cover), (above_in, above), (beneath_in, beneath),
            (sea.at[:, 1], raw_sea.at[1]),
        ])
    ]
    loads[0].start()
    loads[14].start()
    loads[18].start()

    barrier = pltpu.get_barrier_semaphore()

    def greet(n, c):
        pl.semaphore_signal(barrier, inc=1, device_id=at(a + n, half_a), device_id_type=MESH)
        return c

    lax.fori_loop(1, na, greet, 0)

    @pl.when(jnp.logical_not(mine))
    def _():
        pl.semaphore_signal(barrier, inc=1, device_id=at(a, half_a), device_id_type=MESH)

    for di, dj in SIDES:
        pl.semaphore_signal(barrier, inc=1, device_id=at(a + dj, o + di), device_id_type=MESH)

    for load in loads[1:14] + loads[15:18]:
        load.start()

    lane = lax.broadcasted_iota(jnp.int32, (no, 128), 1)

    def pool_table(cell, c):
        row, col = cell // 8, lax.rem(cell, 8)
        flag = jnp.full((no, 256), sea_flag[row, col], jnp.int32).astype(F32)
        r0, c0 = row // 2 * 2, col // 2 * 2
        count = sea_flag[r0, c0] + sea_flag[r0, c0 + 1] + sea_flag[r0 + 1, c0] + sea_flag[r0 + 1, c0 + 1]
        count = jnp.full((no, 256), count, jnp.int32).astype(F32)
        seaw[cell] = 0.5 * flag
        poolw[cell] = flag / jnp.maximum(count, 1.0)
        return c

    loads[14].wait()
    lax.fori_loop(0, 32, pool_table, 0)

    def cell_table(cell, c):
        row, col = cell // 8, lax.rem(cell, 8)
        share = jnp.zeros((no, 128), F32)
        for k in range(4):
            share = share + jnp.where(lane // 16 == cover[row, k, col], 0.25, 0.0)
        cellw[cell] = share
        return c

    def open_sea(par):
        loads[18 * par].wait()
        for w in range(2):
            part = raw_sea[par, :, :, :, 128 * w : 128 * w + 128].astype(F32)
            tok_sea[par, w] = part.reshape(32 * no, 128)

    def sort_sea(par):
        open_sea(par)

        def sort_cell(cell, c):
            row, col = cell // 8, lax.rem(cell, 8)
            for w in range(2):
                part = tok_sea[par, w, pl.ds(cell, no, stride=32), :]
                ocean[0, par, 1 + row, 1 + col, :, 128 * w : 128 * w + 128] = part.astype(BF16)
            return c

        lax.fori_loop(0, 32, sort_cell, 0)

    loads[2].wait()
    sst_wide[...] = lax.dot_general(
        v_to_sst[...], spread_over_lanes(8, 128), (((0,), (0,)), ((), ())), preferred_element_type=F32
    ).astype(BF16)

    def put_air(step, par):
        return [
            pltpu.make_async_remote_copy(
                src_ref=air.at[step, par], dst_ref=there.at[step, par], send_sem=air_send.at[step, par, n],
                recv_sem=air_recv.at[step, par, n], device_id=at(a + da, o), device_id_type=MESH,
            )
            for n, (there, da) in enumerate([(up, 1), (down, -1)])
        ]

    def put_cols(step, par):
        return [
            pltpu.make_async_remote_copy(
                src_ref=ocean.at[step, par, pl.ds(1, 4), src], dst_ref=ocean.at[step, par, pl.ds(1, 4), dst],
                send_sem=sea_send.at[step, par, n], recv_sem=sea_recv.at[step, par, n],
                device_id=at(a + da, o), device_id_type=MESH,
            )
            for n, (src, dst, da) in enumerate([(8, 0, 1), (1, 9, -1)])
        ]

    def put_rows(step, par):
        return [
            pltpu.make_async_remote_copy(
                src_ref=share_tx.at[step, par, n], dst_ref=share_rx.at[step, par, n],
                send_sem=sea_send.at[step, par, 2 + n], recv_sem=sea_recv.at[step, par, 2 + n],
                device_id=at(a, o + do), device_id_type=MESH,
            )
            for n, do in enumerate([1, -1])
        ]

    def send_rows(step, par):
        for copy in put_cols(step, par):
            copy.wait_recv()
        for n, (row, i) in enumerate([(4, 0), (1, 2)]):
            for w in range(2):
                part = slice(128 * w, 128 * w + 128)
                cells = ocean[step, par, row, :, :, part].astype(F32)
                z = jnp.zeros((8, no, 128), F32)
                for j in range(3):
                    z = z + v_sea_filter[3 * i + j : 3 * i + j + 1, part][None] * cells[j : j + 8]
                share_tx[step, par, n, :, :, part] = z.astype(BF16)
        start(put_rows(step, par))

    def start(copies):
        for copy in copies:
            copy.start()

    def make_sst(step, par):
        def block_rows(rr, c):
            parts = []
            for cc in range(4):
                sums = jnp.zeros((no, 256), F32)
                for i in range(2):
                    for j in range(2):
                        cell = (2 * rr + i) * 8 + 2 * cc + j
                        sums = sums + poolw[cell] * ocean[step, par, 1 + 2 * rr + i, 1 + 2 * cc + j].astype(F32)
                parts.append(sums.astype(BF16))
            lines = jnp.zeros((no, 128), F32)
            which = lax.rem(lane // 8, 4)
            for cc in range(4):
                got = jnp.dot(parts[cc], sst_wide[...], preferred_element_type=F32)
                lines = jnp.where(which == cc, got, lines)
            sst_tx[step, par, pl.ds(rr * no, no)] = lines.reshape(no, 1, 128)
            return c

        for rr in range(2):
            block_rows(rr, 0)

    def send_sst(step, par):
        def put(ocn, rr):
            return pltpu.make_async_remote_copy(
                src_ref=sst_tx.at[step, par, rr * no + ocn], dst_ref=sst_rx.at[step, par, a],
                send_sem=sst_send.at[step, par], recv_sem=sst_recv.at[step, par],
                device_id=at(2 * o + rr, ocn), device_id_type=MESH,
            )

        apart = min(4, no)
        for d in sorted(range(apart), key=lambda d: -min(d, apart - d)):
            def put_group(y, c, d=d):
                ocn = y * apart + lax.rem(o + d, apart)
                if d:
                    for rr in range(2):
                        put(ocn, rr).start()
                else:
                    for rr in range(2):
                        @pl.when(jnp.logical_not(is_me(2 * o + rr, ocn)))
                        def _():
                            put(ocn, rr).start()
                return c

            lax.fori_loop(0, no // apart, put_group, 0)

        @pl.when(mine)
        def _():
            pltpu.make_async_copy(
                sst_tx.at[step, par, lax.rem(a, 2) * no + o], sst_rx.at[step, par, a], self_sem.at[step, par, 0]
            ).start()

    def send_flux(step, par):
        place = lax.rem(a, 2) * no + o

        def put(atm):
            atm = lax.rem(atm + na, na)
            return pltpu.make_async_remote_copy(
                src_ref=flux_tx.at[step, par, atm], dst_ref=flux_rx.at[step, par, place],
                send_sem=flux_send.at[step, par], recv_sem=flux_recv.at[step, par],
                device_id=at(atm, half_a), device_id_type=MESH,
            )

        put(a + na // 2).start()

        def put_pair(n, c):
            put(a + na // 2 + n).start()
            put(a + na // 2 - n).start()
            return c

        lax.fori_loop(1, na // 2, put_pair, 0)

        @pl.when(jnp.logical_not(mine))
        def _():
            put(a).start()

        @pl.when(mine)
        def _():
            pltpu.make_async_copy(
                flux_tx.at[step, par, a], flux_rx.at[step, par, place], self_sem.at[step, par, 1]
            ).start()

    def rows_of(buf, sem_send, sem_recv, step, par, count):
        part = buf.at[step, par, pl.ds(0, count)]
        return pltpu.make_async_remote_copy(
            src_ref=part, dst_ref=part, send_sem=sem_send.at[step, par], recv_sem=sem_recv.at[step, par],
            device_id=at(a, o), device_id_type=MESH,
        )

    def exchange_wait(buf, sem_send, sem_recv, step, par, n, received):
        @pl.when(mine)
        def _():
            copy = rows_of(buf, sem_send, sem_recv, step, par, na - 1)
            if received:
                pltpu.make_async_copy(buf.at[step, par, 0], buf.at[step, par, 0], self_sem.at[step, par, n]).wait()
                copy.wait_recv()
            else:
                copy.wait_send()

        @pl.when(jnp.logical_not(mine))
        def _():
            copy = rows_of(buf, sem_send, sem_recv, step, par, na)
            if received:
                copy.wait_recv()
            else:
                copy.wait_send()


    sort_sea(0)
    make_sst(0, 0)

    @pl.when(mine)
    def _():
        pl.semaphore_wait(barrier, na + 3)

    @pl.when(jnp.logical_not(mine))
    def _():
        pl.semaphore_wait(barrier, na + 4)

    send_sst(0, 0)
    sort_sea(1)
    make_sst(0, 1)
    send_sst(0, 1)
    loads[1].wait()
    for w in range(4):
        tok_sky[w] = raw_sky[:, :, :, 128 * w : 128 * w + 128].astype(F32).reshape(8 * na, 128)

    def sort_sky(cc, c):
        for par in range(2):
            for w in range(4):
                part = tok_sky[w, pl.ds(par * 4 * na + cc, na, stride=4), :]
                air[0, par, cc, :, 128 * w : 128 * w + 128] = part.astype(BF16)
        return c

    lax.fori_loop(0, 4, sort_sky, 0)

    for par in range(2):
        start(put_cols(0, par))
        start(put_air(0, par))

    loads[15].wait()
    lax.fori_loop(0, 32, cell_table, 0)

    for load in loads[3:14] + loads[16:18]:
        load.wait()
    flux_wide[...] = lax.dot_general(
        v_to_flux[...], spread_over_lanes(16, 128), (((0,), (0,)), ((), ())), preferred_element_type=F32
    ).astype(BF16)
    heat_wide[...] = lax.dot_general(
        spread_over_lanes(8, 128), v_heat[...].astype(BF16), (((0,), (0,)), ((), ())), preferred_element_type=F32
    ).astype(BF16)
    into_wide[...] = lax.dot_general(
        spread_over_lanes(16, 128), v_from_flux[...].astype(BF16), (((0,), (0,)), ((), ())), preferred_element_type=F32
    ).astype(BF16)

    send_rows(0, 0)

    turns = []
    for code in (above[0], beneath[0]):
        cosine = jnp.where(code == 0, 1.0, 0.0) - jnp.where(code == 2, 1.0, 0.0)
        sine = jnp.where(code == 1, 1.0, 0.0) - jnp.where(code == 3, 1.0, 0.0)
        turns.append((cosine, sine))

    lane_a = lax.broadcasted_iota(jnp.int32, (na, 128), 1)

    def sky_stencil(step, par):
        for copy in put_air(step, par):
            copy.wait_recv()

        def frame(cc, c):
            ext[1, cc + 1] = air[step, par, cc].astype(F32)
            for n, src in ((0, up), (2, down)):
                cosine, sine = turns[n // 2]
                east = src[step, par, cc, :, :256].astype(F32)
                north = src[step, par, cc, :, 256:].astype(F32)
                ext[n, cc + 1, :, :256] = cosine * east - sine * north
                ext[n, cc + 1, :, 256:] = sine * east + cosine * north
            return c

        lax.fori_loop(0, 4, frame, 0)

        def ends(n, c):
            ext[n, 0] = pltpu.roll(ext[n, 4], 1, 0)
            ext[n, 5] = pltpu.roll(ext[n, 1], na - 1, 0)
            return c

        lax.fori_loop(0, 3, ends, 0)

        def column(cc, c):
            for w in range(2):
                part = slice(256 * w, 256 * w + 256)
                z = jnp.zeros((na, 256), F32)
                for i in range(3):
                    for j in range(3):
                        z = z + v_sky_filter[3 * i + j : 3 * i + j + 1, part] * ext[i, cc + j, :, part]
                zbuf[par, cc, :, part] = z
            return c

        lax.fori_loop(0, 4, column, 0)

    def sky_part(step, par):
        exchange_wait(sst_rx, sst_send, sst_recv, step, par, 0, True)
        fields = sst_rx[step, par].reshape(na, 128)
        lhs = [jnp.where(lane_a // 8 == cc, fields, 0.0).astype(BF16) for cc in range(4)]
        warm = jnp.dot(jnp.concatenate(lhs, axis=0), heat_wide[...], preferred_element_type=F32)
        ubuf[...] = normed(warm + zbuf[par].reshape(4 * na, 512), v_sky_gain[...])
        for n in range(4):
            part = slice(256 * n, 256 * n + 256)
            hbuf[:, part] = gelu_twice(jnp.dot(ubuf[...], v_sky_in[:, part], preferred_element_type=F32)).astype(BF16)
        for n in range(2):
            part = slice(256 * n, 256 * n + 256)
            change = 0.5 * jnp.dot(hbuf[...], v_sky_back[:, part], preferred_element_type=F32)
            old = air[step, par, :, :, part].astype(F32)
            air[step + 1, par, :, :, part] = (old + change.reshape(4, na, 256)).astype(BF16)
        lines = jnp.zeros((na, 128), F32)
        for cc in range(4):
            got = jnp.dot(air[step + 1, par, cc], flux_wide[...], preferred_element_type=F32)
            lines = jnp.where(lax.rem(lane_a // 16, 4) == cc, got, lines)
        flux_tx[step, par] = lines.reshape(na, 1, 128)
        send_flux(step, par)

        @pl.when(step + 1 == NSTEP)
        def _():
            def unsort(cc, c):
                for w in range(4):
                    part = air[step + 1, par, cc, :, 128 * w : 128 * w + 128].astype(F32)
                    tok_sky[w, pl.ds(par * 4 * na + cc, na, stride=4), :] = part
                return c

            lax.fori_loop(0, 4, unsort, 0)
            rows = pl.ds(pl.multiple_of(par * 4 * na, 4 * na), 4 * na)
            for w in range(4):
                raw_sky[par, 0, :, 128 * w : 128 * w + 128] = tok_sky[w, rows, :].astype(BF16)
            pltpu.make_async_copy(raw_sky.at[par], sky_out.at[par], out_sem.at[par]).start()

    def sea_line(step, par, row, taps, side):
        for w in range(2):
            part = slice(128 * w, 128 * w + 128)
            z = jnp.zeros((8, no, 128), F32) if side is None else share_rx[step, par, side, :, :, part].astype(F32)
            for i in taps:
                cells = ocean[step, par, row + i, :, :, part].astype(F32)
                for j in range(3):
                    z = z + v_sea_filter[3 * i + j : 3 * i + j + 1, part][None] * cells[j : j + 8]
            zsea[par, row, :, part] = z.reshape(8 * no, 128)

    def sea_middle(step, par):
        def line(row, c):
            sea_line(step, par, row, (0, 1, 2), None)
            return c

        lax.fori_loop(1, 3, line, 0)

    def sea_edges(step, par):
        for copy in put_rows(step, par):
            copy.wait_recv()
        sea_line(step, par, 0, (1, 2), 0)
        sea_line(step, par, 3, (0, 1), 1)

    def sea_part(step, par):
        exchange_wait(flux_rx, flux_send, flux_recv, step, par, 1, True)
        got = flux_rx[step, par].reshape(2 * no, 128)
        fields = jnp.where(lane < 64, got[:no], got[no:])
        rows = 16 * no
        for m in range(2):
            lhs = (cellw[16 * m : 16 * m + 16] * fields[None]).astype(BF16).reshape(rows, 128)
            forced = jnp.dot(lhs, into_wide[...], preferred_element_type=F32)
            z = forced + zsea[par, 2 * m : 2 * m + 2].reshape(rows, 256)
            usea[rows * m : rows * m + rows] = normed(z, v_sea_gain[...])
        for m in range(2):
            for n in range(2):
                part = slice(256 * n, 256 * n + 256)
                got = jnp.dot(usea[rows * m : rows * m + rows], v_sea_in[:, part], preferred_element_type=F32)
                hsea[rows * m : rows * m + rows, part] = gelu_twice(got).astype(BF16)
        for m in range(2):
            change = jnp.dot(hsea[rows * m : rows * m + rows], v_sea_back[...], preferred_element_type=F32)
            change = change.reshape(2, 8, no, 256) * seaw[16 * m : 16 * m + 16].reshape(2, 8, no, 256)
            old = ocean[step, par, 1 + 2 * m : 3 + 2 * m, 1:9].astype(F32)
            ocean[step + 1, par, 1 + 2 * m : 3 + 2 * m, 1:9] = (old + change).astype(BF16)

        @pl.when(step + 1 < NSTEP)
        def _():
            make_sst(step + 1, par)
            send_sst(step + 1, par)
            start(put_cols(step + 1, par))

        @pl.when(step + 1 == NSTEP)
        def _():
            pltpu.make_async_copy(
                ocean.at[step + 1, par, pl.ds(1, 4), pl.ds(1, 8)], sea_out.at[par], out_sem.at[2 + par]
            ).start()

    def both(step, *parts):
        def run(par, c):
            for part in parts:
                part(step, par)
            return c

        lax.fori_loop(0, 2, run, 0)

    def one_step(step, c):
        both(step, sky_stencil)
        both(step, sky_part)

        send_rows(step, 1)

        @pl.when(step + 1 < NSTEP)
        def _():
            for par in range(2):
                start(put_air(step + 1, par))

        both(step, sea_middle)
        both(step, sea_edges, sea_part)

        @pl.when(step + 1 < NSTEP)
        def _():
            send_rows(step + 1, 0)

        return c

    lax.fori_loop(0, NSTEP, one_step, 0)

    def close(n, c):
        step, par = n // 2, lax.rem(n, 2)
        for copy in put_air(step, par) + put_cols(step, par) + put_rows(step, par):
            copy.wait_send()
        exchange_wait(sst_tx, sst_send, sst_recv, step, par, 0, False)
        exchange_wait(flux_tx, flux_send, flux_recv, step, par, 1, False)
        return c

    lax.fori_loop(0, 2 * NSTEP, close, 0)
    for par in range(2):
        pltpu.make_async_copy(raw_sky.at[par], sky_out.at[par], out_sem.at[par]).wait()
        pltpu.make_async_copy(
            ocean.at[NSTEP, par, pl.ds(1, 4), pl.ds(1, 8)], sea_out.at[par], out_sem.at[2 + par]
        ).wait()


def local(na, no, sky, sea, above, beneath, cover, sea_flag, sky_filter, sky_gain, heat, sky_in, sky_back, to_flux,
          sea_filter, sea_gain, from_flux, sea_in, sea_back, to_sst):
    hbm = pl.BlockSpec(memory_space=pl.ANY)
    vmem = pltpu.VMEM
    dma = pltpu.SemaphoreType.DMA
    n, p = NSTEP, 2
    big = [sky, sea.reshape(no, 2, *sea.shape[1:]), sky_filter, sky_gain[None], heat, sky_in, sky_back, to_flux.T, sea_filter, sea_gain[None], from_flux, sea_in,
           sea_back, to_sst.T]
    small = [above, beneath, cover.transpose(0, 2, 1), sea_flag]
    sky_new, sea_new = pl.pallas_call(
        functools.partial(kernel, na, no),
        out_shape=(
            jax.ShapeDtypeStruct(sky.shape, BF16),
            jax.ShapeDtypeStruct((p, 4, 8, no, 256), BF16),
        ),
        in_specs=[hbm] * (4 + len(big)),
        out_specs=(hbm, hbm),
        scratch_shapes=[pltpu.SMEM(x.shape, x.dtype) for x in small] + [vmem(x.shape, x.dtype) for x in big[:1]] + [
            vmem((2, no, *sea.shape[1:]), BF16)
        ] + [vmem(x.shape, x.dtype) for x in big[2:]] + [
            vmem((4, p * 4 * na, 128), F32),
            vmem((2, 2, no * 32, 128), F32),
            vmem((n + 1, p, 4, na, 512), BF16),
            vmem((n, p, 4, na, 512), BF16),
            vmem((n, p, 4, na, 512), BF16),
            vmem((n + 1, p, 6, 10, no, 256), BF16),
            vmem((n, p, 2, 8, no, 256), BF16),
            vmem((n, p, 2, 8, no, 256), BF16),
            vmem((3, 6, na, 512), F32),
            vmem((p, 4, na, 512), F32),
            vmem((4 * na, 512), BF16),
            vmem((4 * na, 1024), BF16),
            vmem((p, 4, 8 * no, 256), F32),
            vmem((32 * no, 256), BF16),
            vmem((32 * no, 512), BF16),
            vmem((512, 128), BF16),
            vmem((128, 512), BF16),
            vmem((128, 256), BF16),
            vmem((256, 128), BF16),
            vmem((32, no, 128), F32),
            vmem((32, no, 256), F32),
            vmem((32, no, 256), F32),
            vmem((n, p, na, 1, 128), F32),
            vmem((n, p, na, 1, 128), F32),
            vmem((n, p, na, 1, 128), F32),
            vmem((n, p, na, 1, 128), F32),
            dma((len(small) + len(big) + 1,)),
            dma((n, p)),
            dma((n, p)),
            dma((n, p)),
            dma((n, p)),
            dma((n, p, 2)),
            dma((n, p, 2)),
            dma((n, p, 2)),
            dma((n, p, 4)),
            dma((n, p, 4)),
            dma((4,)),
        ],
        compiler_params=pltpu.CompilerParams(
            collective_id=0, has_side_effects=True, vmem_limit_bytes=56 * 1024 * 1024
        ),
        name="coupled_steps",
    )(*small, *big)
    sea_new = sea_new.transpose(3, 0, 1, 2, 4).reshape(sea.shape)
    return sky_new, sea_new


def solution(mesh):
    return jax.shard_map(
        functools.partial(local, mesh.shape["atm"], mesh.shape["ocn"]),
        mesh=mesh,
        in_specs=(
            P("ocn", "atm", None, None),
            P(None, "ocn", "atm", None),
            P("atm"),
            P("atm"),
            P("ocn", "atm", None),
            P("ocn", "atm"),
        ) + (P(),) * 12,
        out_specs=(P("ocn", "atm", None, None), P(None, "ocn", "atm", None)),
        check_vma=False,
    )
```
